32 devices in a mesh: ctx: 8 (over z, x), head: 4 (over y, core).
Axes of the slice: x: 2, y: 2, z: 4, core: 2. Of those that a mesh axis runs over, the one named last changes fastest.
Arguments:
- queries: bfloat16 [4096, 8192], P('ctx', 'head'), may hold values from -6 to 6
- key_rows: bfloat16 [4096, 8192], P('ctx', 'head'), may hold values from -8 to 8
- value_rows: bfloat16 [4096, 8192], P('ctx', 'head'), may hold values from -6 to 6
- log_decay: float32 [4096, 64], P('ctx', 'head'), may hold values from -3 to 0, as said below
- write_rate: float32 [4096, 64], P('ctx', 'head'), may hold values from 0 to 1, as said below
- level_weights: float32 [4096, 320], P('ctx', 'head'), may hold values from 0.25 to 2.5
- block_levels: int32 [64], P('ctx'), may hold values from 1 to 5
Outputs:
- mixed: bfloat16 [4096, 8192], P(('ctx', 'head'))
The draws below stay inside these ranges and needn't reach their ends.
Inputs may be any that keep to these rules, and one draw needn't show every extreme that they name: `log_decay`: strictly negative. `write_rate`: strictly positive.
All inputs are finite; a program needn't handle non-finite values.
Results may differ from the reference program's by a relative error of at most 0.0087.
Values may be sent and summed in bfloat16 or wider, within the bound.
No kernel may reach another device: no remote copies, remote signals or barrier semaphores. Data moves between devices by JAX's collectives and lax.ppermute only.
A program may use at most 128 MiB of HBM per device.

```python
import math
import jax
import jax.numpy as jnp
from jax import lax

HEAD_TOTAL = 64
D_HEAD = 128
TOK_DEV = 512
BLOCK = 64
LEVELS = 5
TOKEN_TOTAL = 4096
N_CTX = 8


def head_plan(key):
    base_key = jax.random.fold_in(key, 4242)
    share_slow = 0.5
    return jax.random.uniform(jax.random.fold_in(base_key, 1), (HEAD_TOTAL,)) < share_slow


def drawn_plan(key):
    plan_key = jax.random.fold_in(key, 5151)
    block_count = TOKEN_TOTAL // BLOCK
    per_shard = TOK_DEV // BLOCK
    chosen = jax.random.uniform(jax.random.fold_in(plan_key, 1), (block_count,)) < 1.0 / 6.0
    forced = jax.random.randint(jax.random.fold_in(plan_key, 2), (block_count // per_shard,), 0, per_shard)
    block_ids = jnp.arange(block_count)
    forced_hit = block_ids % per_shard == jnp.repeat(forced, per_shard)
    return jnp.logical_or(chosen, forced_hit)


def log_between(key, shape, lower_end, upper_end):
    return jnp.exp(jax.random.uniform(key, shape, jnp.float32, jnp.log(lower_end), jnp.log(upper_end)))


def draw_key_rows(key, part):
    aligned = drawn_plan(key)
    block_count = TOKEN_TOTAL // BLOCK
    feature_count = HEAD_TOTAL * D_HEAD
    shared = jax.random.normal(jax.random.fold_in(key, 31), (block_count, 1, feature_count), jnp.float32)
    noise = jax.random.normal(jax.random.fold_in(key, 32), (block_count, BLOCK, feature_count), jnp.float32)
    values = jnp.where(aligned[:, None, None], shared + 0.5 * noise, noise)
    return jnp.clip(values, -8.0, 8.0).reshape(TOKEN_TOTAL, feature_count).astype(jnp.bfloat16)


def draw_log_decay(key, part):
    slow_heads = head_plan(key)
    slow_rate = log_between(jax.random.fold_in(key, 11), (HEAD_TOTAL,), 0.2, 1.0) / TOKEN_TOTAL
    fast_rate = log_between(jax.random.fold_in(key, 12), (HEAD_TOTAL,), 1.0 / 50.0, 1.0 / 25.0)
    head_decay_rate = jnp.where(slow_heads, slow_rate, fast_rate)
    approximate = log_between(jax.random.fold_in(key, 13), (TOKEN_TOTAL, HEAD_TOTAL), 0.5, 2.0)
    segment_position = jax.random.randint(jax.random.fold_in(key, 14), (4, HEAD_TOTAL), 0, TOKEN_TOTAL)
    segment_length = jax.random.uniform(jax.random.fold_in(key, 15), (4, HEAD_TOTAL), jnp.float32, 0.22, 0.69)
    match_count = jnp.arange(TOKEN_TOTAL)[:, None, None] == segment_position[None]
    segments = jnp.sum(jnp.where(match_count, segment_length[None], 0.0), axis=1)
    return -(head_decay_rate[None, :] * approximate) - segments


def draw_write_rate(key, part):
    slow_heads = head_plan(key)
    aligned = drawn_plan(key)
    block_count = TOKEN_TOTAL // BLOCK
    slow_scale = log_between(jax.random.fold_in(key, 21), (HEAD_TOTAL,), 0.5, 2.0) * 64.0 / TOKEN_TOTAL
    fast_scale = log_between(jax.random.fold_in(key, 22), (HEAD_TOTAL,), 0.1, 0.45)
    head_scale = jnp.where(slow_heads, slow_scale, fast_scale)
    approximate = log_between(jax.random.fold_in(key, 23), (TOKEN_TOTAL, HEAD_TOTAL), 0.5, 2.0)
    base_rate = (head_scale[None, :] * approximate).reshape(block_count, BLOCK, HEAD_TOTAL)
    strong_heads = jax.random.uniform(jax.random.fold_in(key, 24), (block_count, HEAD_TOTAL)) < 0.5
    strong_rate = log_between(jax.random.fold_in(key, 25), (block_count, BLOCK, HEAD_TOTAL), 0.3, 0.9)
    strong_mask = jnp.logical_and(aligned[:, None], strong_heads)
    rate = jnp.where(strong_mask[:, None, :], strong_rate, base_rate)
    return jnp.minimum(rate, 1.0).reshape(TOKEN_TOTAL, HEAD_TOTAL)


def with_ends(entries, own_key, smallest, largest):
    longest = entries.shape.index(max(entries.shape))
    spots = []
    for shift in (0, 1):
        where = [jax.random.randint(jax.random.fold_in(own_key, axis), (), 0, length) for axis, length in enumerate(entries.shape)]
        where[longest] = (where[longest] + shift) % entries.shape[longest]
        spots.append(tuple(where))
    return entries.at[spots[0]].set(smallest).at[spots[1]].set(largest)


def block_scale(own_key, shape, cuts, least, top_value):
    level = 1.0
    for dim, parts in cuts:
        draws = jax.random.uniform(jax.random.fold_in(jax.random.fold_in(own_key, 6), dim), (parts,), jnp.float32, least / len(cuts), top_value / len(cuts))
        level = level * jnp.repeat(jnp.exp(draws), shape[dim] // parts).reshape((-1,) + (1,) * (len(shape) - 1 - dim))
    return level


def gaussian(key, shape, scale, reach, split=(), kind=jnp.bfloat16):
    loudness = block_scale(key, shape, split, -0.22, 0.18) if split else 1.0
    values = jax.random.normal(key, shape, jnp.float32) * scale * loudness
    return jnp.minimum(jnp.maximum(values, -reach), reach).astype(kind)


def setup_inputs(seed: int = 0) -> dict:
    arg_keys = jax.random.split(jax.random.key(seed), 8)
    queries = gaussian(arg_keys[0], (TOKEN_TOTAL, HEAD_TOTAL * D_HEAD), 1.0, 6.0, ((0, 8), (1, 4)))
    key_rows = draw_key_rows(jax.random.fold_in(arg_keys[7], 71), 0)
    value_rows = gaussian(arg_keys[2], (TOKEN_TOTAL, HEAD_TOTAL * D_HEAD), 1.0, 6.0, ((0, 8), (1, 4)))
    log_decay = draw_log_decay(jax.random.fold_in(arg_keys[7], 71), 0)
    write_rate = draw_write_rate(jax.random.fold_in(arg_keys[7], 71), 0)
    level_weights = jnp.clip(jnp.exp(math.log(2.5) - 2.3025851 * jax.random.uniform(arg_keys[5], (TOKEN_TOTAL, HEAD_TOTAL * LEVELS), jnp.float32) ** block_scale(arg_keys[5], (TOKEN_TOTAL, HEAD_TOTAL * LEVELS), ((0, 8), (1, 4)), -0.2, 0.2)), 0.25, 2.5)
    block_levels = with_ends(jax.random.randint(arg_keys[6], (TOKEN_TOTAL // BLOCK,), 1, LEVELS + 1), jax.random.fold_in(arg_keys[6], 1), 1, LEVELS).astype(jnp.int32)
    return dict(queries=queries, key_rows=key_rows, value_rows=value_rows, log_decay=log_decay, write_rate=write_rate, level_weights=level_weights, block_levels=block_levels)


precise = lax.Precision.HIGHEST

def matmul_hi(left_mat, right_mat):
    return jnp.matmul(left_mat, right_mat, precision=precise)

def low_product(form, left_op, right_op):
    return jnp.einsum(form, left_op.astype(jnp.float32), right_op.astype(jnp.float32), precision=precise)

def to_blocks(tensor):
    block_count = tensor.shape[0] // BLOCK
    shaped = tensor.reshape((block_count, BLOCK) + tensor.shape[1:])
    return jnp.moveaxis(shaped, 2, 0)

def prepare(query_in, key_in, value_in, head_count):
    length = query_in.shape[0]
    query_low = query_in.reshape(length, head_count, -1)
    key_f = key_in.astype(jnp.float32).reshape(length, head_count, -1)
    key_low = (key_f * lax.rsqrt(lax.optimization_barrier(jnp.sum(key_f * key_f, axis=-1, keepdims=True)) + 1e-06)).astype(jnp.bfloat16)
    value_f = value_in.astype(jnp.float32).reshape(length, head_count, -1)
    return (query_low, key_low, value_f)

def local_pass(query_low, key_low, value_f, log_decay, write_rate):
    head_count = key_low.shape[1]
    head_width = key_low.shape[2]
    query_b = to_blocks(query_low)
    key_lb = to_blocks(key_low)
    key_b = key_lb.astype(jnp.float32)
    value_b = to_blocks(value_f)
    cum_log = jnp.cumsum(to_blocks(log_decay), axis=-1)
    rate_b = to_blocks(write_rate)
    places = jnp.arange(BLOCK)
    lower_tri = places[:, None] >= places[None, :]
    strict_tri = places[:, None] > places[None, :]
    log_gaps = cum_log[..., :, None] - cum_log[..., None, :]
    decay_incl = jnp.exp(jnp.where(lower_tri, log_gaps, -1e+30))
    decay_strict = jnp.where(strict_tri, decay_incl, 0.0)
    gram_keys = jnp.einsum('hbik,hbjk->hbij', key_b, key_b, precision=precise)
    strict_part = rate_b[..., :, None] * decay_strict * gram_keys
    right_side = jnp.concatenate([rate_b[..., None] * value_b, (rate_b * jnp.exp(cum_log))[..., None] * key_b], axis=-1)
    solved = jax.scipy.linalg.solve_triangular(strict_part, right_side, lower=True, unit_diagonal=True)
    wy_values = solved[..., :head_width]
    wy_keys = solved[..., head_width:]
    inputs = jnp.concatenate([wy_values, jnp.zeros_like(wy_keys)], axis=-1)
    key_tail = jnp.exp(cum_log[..., -1:] - cum_log)[..., None] * key_b
    block_fall = jnp.exp(cum_log[..., -1])
    scores_low = (low_product('hbik,hbjk->hbij', query_b, key_lb) * decay_incl).astype(jnp.bfloat16)
    initial = jnp.concatenate([jnp.zeros((head_count, head_width, head_width), key_b.dtype), jnp.broadcast_to(jnp.eye(head_width, dtype=key_b.dtype), (head_count, head_width, head_width))], axis=-1)

    def advance(carry_state, slices):
        wy_part, given_vals, tail_keys, fall_now = slices
        errors = given_vals - jnp.einsum('hcd,hde->hce', wy_part, carry_state, precision=precise)
        updated = fall_now[:, None, None] * carry_state + jnp.einsum('hcd,hce->hde', tail_keys, errors, precision=precise)
        return (updated, (carry_state, errors))
    end_state, (starts, errors) = lax.scan(advance, initial, (jnp.moveaxis(wy_keys, 1, 0), jnp.moveaxis(inputs, 1, 0), jnp.moveaxis(key_tail, 1, 0), jnp.moveaxis(block_fall, 1, 0)))
    mixed = jnp.exp(cum_log)[..., None] * low_product('hbcd,bhde->hbce', query_b, starts.astype(jnp.bfloat16))
    mixed = mixed + low_product('hbij,bhje->hbie', scores_low, errors.astype(jnp.bfloat16))
    mixed = jnp.moveaxis(mixed, 0, 2).reshape(-1, head_count, 2 * head_width)
    return (mixed, end_state)

def join_runs(left_run, right_run):
    head_width = left_run.shape[-2]
    return matmul_hi(right_run[..., head_width:], left_run) + jnp.concatenate([right_run[..., :head_width], jnp.zeros_like(right_run[..., :head_width])], axis=-1)

def finish(mixed, carried, weights, levels_in):
    length, head_count, twice = mixed.shape
    head_width = twice // 2
    near_part = mixed[..., :head_width]
    row_part = mixed[..., head_width:].astype(jnp.bfloat16)
    far_part = low_product('thd,lhde->thle', row_part, carried.astype(jnp.bfloat16))
    terms = jnp.concatenate([near_part[:, :, None], far_part], axis=2)
    level_ids = jnp.arange(LEVELS)
    keep_mask = (level_ids[None, :] < levels_in[:, None]).astype(weights.dtype)
    scaled = weights.reshape(length // BLOCK, BLOCK, head_count, LEVELS) * keep_mask[:, None, None, :]
    scaled = scaled.reshape(length, head_count, LEVELS)
    total = lax.optimization_barrier(jnp.sum(scaled[..., None] * terms, axis=2))
    return total.astype(jnp.bfloat16).reshape(length, head_count * head_width)

def reference(queries, key_rows, value_rows, log_decay, write_rate, level_weights, block_levels):

    def shard_local(shard_id):
        first = shard_id * TOK_DEV
        query_low, key_low, value_f = prepare(lax.dynamic_slice_in_dim(queries, first, TOK_DEV, 0), lax.dynamic_slice_in_dim(key_rows, first, TOK_DEV, 0), lax.dynamic_slice_in_dim(value_rows, first, TOK_DEV, 0), HEAD_TOTAL)
        return local_pass(query_low, key_low, value_f, lax.dynamic_slice_in_dim(log_decay, first, TOK_DEV, 0), lax.dynamic_slice_in_dim(write_rate, first, TOK_DEV, 0))
    shard_ids = jnp.arange(N_CTX, dtype=jnp.int32)
    mixed_all, run_all = lax.map(shard_local, shard_ids)
    head_width = D_HEAD
    prefix = jnp.broadcast_to(jnp.eye(head_width, dtype=run_all.dtype), run_all.shape[:2] + (head_width, head_width))
    bits_total = N_CTX.bit_length() - 1
    carried = []
    for section in range(bits_total):
        sibling = shard_ids >> section ^ 1
        upper = (shard_ids >> section & 1 == 1)[:, None, None, None]
        other_run = jnp.take(run_all, sibling, axis=0)
        carried.append(jnp.where(upper, matmul_hi(prefix, other_run[..., :head_width]), 0.0))
        prefix = jnp.where(upper, matmul_hi(prefix, other_run[..., head_width:]), prefix)
        if section + 1 < bits_total:
            run_all = join_runs(run_all[0::2], run_all[1::2])
    for section in range(bits_total, LEVELS - 1):
        carried.append(jnp.zeros_like(prefix))
    carried = jnp.stack(carried, axis=1)

    def shard_finish(shard_id):
        first = shard_id * TOK_DEV
        return finish(mixed_all[shard_id], carried[shard_id], lax.dynamic_slice_in_dim(level_weights, first, TOK_DEV, 0), lax.dynamic_slice_in_dim(block_levels, shard_id * (TOK_DEV // BLOCK), TOK_DEV // BLOCK, 0))
    outputs = lax.map(shard_finish, shard_ids)
    return outputs.reshape(TOKEN_TOTAL, HEAD_TOTAL * D_HEAD)
```

```python
import jax
import jax.numpy as jnp
from jax import lax
from jax.sharding import PartitionSpec as P
from jax.experimental import pallas as pl
from jax.experimental.pallas import tpu as pltpu

BLOCK = 64
WIDE = 128
LEVELS = 5
f32 = jnp.float32
bf16 = jnp.bfloat16


def mxu(a, b):
    return lax.dot_general(a, b, (((1,), (0,)), ((), ())), preferred_element_type=f32)


def mxu_t(a, b):
    return lax.dot_general(a, b, (((1,), (1,)), ((), ())), preferred_element_type=f32)


def halves(x):
    hi = x.astype(bf16)
    return hi, (x - hi.astype(f32)).astype(bf16)


def local_kernel(
    q_ref, k_ref, v_ref, ld_ref, wr_ref,
    run_ref, near_ref, rows_ref,
    kn_s, gram_s, low_s, inv_s, row_s, colg_s, colb_s, m_s, s_s, qt_s, near_s, p_s,
):
    heads = k_ref.shape[1] // WIDE
    tokens = k_ref.shape[0]
    pairs = tokens // WIDE
    units = heads * pairs
    blocks = tokens // BLOCK

    lane = lax.broadcasted_iota(jnp.int32, (BLOCK, WIDE), 1)
    left = lane < BLOCK
    ri = lax.broadcasted_iota(jnp.int32, (WIDE, WIDE), 0)
    ci = lax.broadcasted_iota(jnp.int32, (WIDE, WIDE), 1)
    tri = jnp.where((ri <= ci) & ((ri >= BLOCK) == (ci >= BLOCK)), 1.0, 0.0)
    grow = lax.dot_general(
        ld_ref[...], tri, (((1,), (0,)), ((), ())),
        precision=lax.Precision.HIGHEST, preferred_element_type=f32,
    )
    row_s[0] = grow
    row_s[1] = jnp.exp(grow)
    gcol = grow.T
    bcol = wr_ref[...].T
    colg_s[...] = jnp.concatenate([gcol[:BLOCK], gcol[BLOCK:]], axis=1)
    colb_s[...] = jnp.concatenate([bcol[:BLOCK], bcol[BLOCK:]], axis=1)

    def keys(h, _):
        cols = pl.ds(pl.multiple_of(h * WIDE, WIDE), WIDE)
        kf = k_ref[:, cols].astype(f32)
        kn = (kf * lax.rsqrt(jnp.sum(kf * kf, axis=1, keepdims=True) + 1e-6)).astype(bf16)
        kn_s[h] = kn
        for p in range(pairs):
            kp = kn[p * WIDE:(p + 1) * WIDE]
            g = mxu_t(kp, kp)
            u = h * pairs + p
            gram_s[pl.ds(pl.multiple_of(u * BLOCK, BLOCK), BLOCK), :] = jnp.where(
                left, g[:BLOCK], g[BLOCK:]
            )
        return 0

    lax.fori_loop(0, heads, keys, 0)

    def to_lanes(i, _):
        a = gram_s[pl.ds(i, units, stride=BLOCK), :].T
        g = jnp.concatenate([a[:BLOCK], a[BLOCK:]], axis=1)
        gi = colg_s[pl.ds(i, 1), :]
        bi = colb_s[pl.ds(i, 1), :]
        low_s[i] = g * (bi * jnp.exp(gi - colg_s[...]))
        inv_s[i] = jnp.zeros_like(g)
        return 0

    lax.fori_loop(0, BLOCK, to_lanes, 0)

    lanes = 2 * units
    sub = lax.broadcasted_iota(jnp.int32, (8, lanes), 0)

    def solve(bi, _):
        i0 = bi * 8

        def column(cb, _):
            c0 = pl.multiple_of(cb * 8, 8)

            def step(jb, acc):
                acc = list(acc)
                for jj in range(8):
                    j = jb * 8 + jj
                    t = inv_s[j, pl.ds(c0, 8), :]
                    for r in range(8):
                        acc[r] = acc[r] - low_s[i0 + r, pl.ds(j, 1), :] * t
                return tuple(acc)

            on = cb == bi
            acc = tuple(jnp.where((sub == r) & on, 1.0, 0.0) for r in range(8))
            acc = list(lax.fori_loop(cb, bi, step, acc))
            for r in range(8):
                inv_s[i0 + r, pl.ds(c0, 8), :] = acc[r]
                for s in range(r + 1, 8):
                    acc[s] = acc[s] - low_s[i0 + s, pl.ds(i0 + r, 1), :] * acc[r]
            return 0

        lax.fori_loop(0, bi + 1, column, 0)
        return 0

    lax.fori_loop(0, BLOCK // 8, solve, 0)

    def from_lanes(i, _):
        t = inv_s[i] * colb_s[...]
        a = jnp.concatenate([t[:, :units], t[:, units:]], axis=0)
        gram_s[pl.ds(i, units, stride=BLOCK), :] = a.T
        return 0

    lax.fori_loop(0, BLOCK, from_lanes, 0)

    clane = lax.broadcasted_iota(jnp.int32, (BLOCK, lanes), 1)
    row64 = lax.broadcasted_iota(jnp.int32, (BLOCK, WIDE), 0)
    keep = row64 >= jnp.where(left, lane, lane - BLOCK)
    eye = ri == ci

    def unit(u, _):
        h = u // pairs
        p = u - h * pairs
        cols = pl.ds(pl.multiple_of(h * WIDE, WIDE), WIDE)
        toks = pl.ds(pl.multiple_of(p * WIDE, WIDE), WIDE)
        grow = row_s[0, pl.ds(u, 1), :]
        erow = row_s[1, pl.ds(u, 1), :]
        g0 = jnp.sum(jnp.where(clane == u, colg_s[...], 0.0), axis=1, keepdims=True)
        g1 = jnp.sum(jnp.where(clane == u + units, colg_s[...], 0.0), axis=1, keepdims=True)
        g0 = jnp.broadcast_to(g0, (BLOCK, WIDE))
        g1 = jnp.broadcast_to(g1, (BLOCK, WIDE))
        q = q_ref[toks, cols]
        kn = kn_s[h, toks, :]
        v = v_ref[toks, cols]
        qk = mxu_t(q, kn)
        decay = jnp.exp(jnp.where(keep, jnp.where(left, g0, g1) - grow, -1e30))
        score = jnp.where(left, qk[:BLOCK], qk[BLOCK:]) * decay
        zero = jnp.zeros_like(score)

        def diagonal(x):
            return jnp.concatenate([jnp.where(left, x, zero), jnp.where(left, zero, x)], axis=0)

        t1 = gram_s[pl.ds(pl.multiple_of(u * BLOCK, BLOCK), BLOCK), :]
        t2 = t1 * erow
        a_hi, a_lo = halves(diagonal(t1))
        b_hi, b_lo = halves(diagonal(t2))
        wv = mxu(jnp.concatenate([a_hi, a_lo], axis=1), jnp.concatenate([v, v], axis=0))
        wk = mxu(jnp.concatenate([b_hi, b_lo], axis=1), jnp.concatenate([kn, kn], axis=0))
        w = jnp.concatenate([wv, wk], axis=1)
        ys = mxu(diagonal(score).astype(bf16), w.astype(bf16))
        near_s[u] = ys[:, :WIDE]
        eg = jnp.exp(jnp.concatenate([g0, g1], axis=0))
        qt_s[u] = (eg * q.astype(f32) - ys[:, WIDE:]).astype(bf16)
        knt = kn.astype(f32).T.astype(bf16)
        kk = jnp.concatenate([knt, knt], axis=1)
        for half, g in enumerate((g0, g1)):
            end = g[BLOCK - 1:, :]
            tail = jnp.exp(end - g)
            part = w[half * BLOCK:(half + 1) * BLOCK] * jnp.concatenate([tail, tail], axis=1)
            hi, lo = halves(part)
            none = jnp.zeros_like(hi)
            stack = [hi, none, lo, none] if half == 0 else [none, hi, none, lo]
            y = mxu(kk, jnp.concatenate(stack, axis=0))
            s_s[2 * u + half] = y[:, :WIDE]
            m = jnp.where(eye, jnp.exp(end), 0.0) - y[:, WIDE:]
            m_hi, m_lo = halves(m)
            m_s[2 * u + half] = jnp.concatenate([m_hi, m_lo], axis=1)
        return 0

    lax.fori_loop(0, units, unit, 0)

    start = jnp.where(eye, 1.0, 0.0)
    for h in range(heads):
        p_s[h] = jnp.concatenate([jnp.zeros_like(start), start], axis=1)

    def scan(b, _):
        toks = pl.ds(pl.multiple_of(b * BLOCK, BLOCK), BLOCK)
        half = pl.ds(pl.multiple_of((b % 2) * BLOCK, BLOCK), BLOCK)
        for h in range(heads):
            u = h * pairs + b // 2
            at = h * blocks + b
            cols = pl.ds(h * WIDE, WIDE)
            p = p_s[h]
            p_hi, p_lo = halves(p)
            o = mxu(qt_s[u, half, :], p_hi)
            near_ref[toks, cols] = near_s[u, half, :] + o[:, :WIDE]
            rows_ref[toks, cols] = o[:, WIDE:].astype(bf16)
            m = m_s[at]
            n = mxu(
                jnp.concatenate([m, m[:, :WIDE]], axis=1),
                jnp.concatenate([p_hi, p_hi, p_lo], axis=0),
            )
            p_s[h] = n + jnp.concatenate([s_s[at], jnp.zeros_like(start)], axis=1)
        return 0

    lax.fori_loop(0, blocks, scan, 0)
    for h in range(heads):
        run_ref[h] = p_s[h].astype(bf16)


def local_call(q, k, v, ldt, wrt, group, heads):
    tokens = q.shape[0]
    units = heads * tokens // WIDE
    big = lambda: pl.BlockSpec((tokens, heads * WIDE), lambda i: (0, group))
    small = lambda: pl.BlockSpec((units, WIDE), lambda i: (group, 0))
    return pl.pallas_call(
        local_kernel,
        grid=(1,),
        in_specs=[big(), big(), big(), small(), small()],
        out_specs=[
            pl.BlockSpec((heads, WIDE, 2 * WIDE), lambda i: (0, 0, 0)),
            pl.BlockSpec((tokens, heads * WIDE), lambda i: (0, 0)),
            pl.BlockSpec((tokens, heads * WIDE), lambda i: (0, 0)),
        ],
        out_shape=[
            jax.ShapeDtypeStruct((heads, WIDE, 2 * WIDE), bf16),
            jax.ShapeDtypeStruct((tokens, heads * WIDE), f32),
            jax.ShapeDtypeStruct((tokens, heads * WIDE), bf16),
        ],
        scratch_shapes=[
            pltpu.VMEM((heads, tokens, WIDE), bf16),
            pltpu.VMEM((units * BLOCK, WIDE), f32),
            pltpu.VMEM((BLOCK, BLOCK, 2 * units), f32),
            pltpu.VMEM((BLOCK, BLOCK, 2 * units), f32),
            pltpu.VMEM((2, units, WIDE), f32),
            pltpu.VMEM((BLOCK, 2 * units), f32),
            pltpu.VMEM((BLOCK, 2 * units), f32),
            pltpu.VMEM((2 * units, WIDE, 2 * WIDE), bf16),
            pltpu.VMEM((2 * units, WIDE, WIDE), f32),
            pltpu.VMEM((units, WIDE, WIDE), bf16),
            pltpu.VMEM((units, WIDE, WIDE), f32),
            pltpu.VMEM((heads, WIDE, 2 * WIDE), f32),
        ],
        compiler_params=pltpu.CompilerParams(vmem_limit_bytes=60 * 1024 * 1024),
        name="local",
    )(q, k, v, ldt, wrt)


def rows_of(x):
    return x.T.reshape(-1, WIDE)


def stage_kernel(flag_ref, own_ref, other_ref, prefix_ref, run_ref, carry_ref, next_ref):
    heads = own_ref.shape[0]

    @pl.when(flag_ref[0] == 1)
    def _():
        for h in range(heads):
            own = own_ref[h]
            other = other_ref[h]
            both = mxu(jnp.concatenate([own[:, WIDE:], prefix_ref[h]], axis=0), other)
            run_ref[h, :, :WIDE] = (both[:WIDE, :WIDE] + own[:, :WIDE].astype(f32)).astype(bf16)
            run_ref[h, :, WIDE:] = both[:WIDE, WIDE:].astype(bf16)
            carry_ref[h] = both[WIDE:, :WIDE].astype(bf16)
            next_ref[h] = both[WIDE:, WIDE:].astype(bf16)

    @pl.when(flag_ref[0] == 0)
    def _():
        for h in range(heads):
            own = own_ref[h]
            other = other_ref[h]
            both = mxu(other[:, WIDE:], own)
            run_ref[h, :, :WIDE] = (both[:, :WIDE] + other[:, :WIDE].astype(f32)).astype(bf16)
            run_ref[h, :, WIDE:] = both[:, WIDE:].astype(bf16)
            carry_ref[h] = jnp.zeros((WIDE, WIDE), bf16)
            next_ref[h] = prefix_ref[h]


def stage_call(flag, own, other, prefix):
    heads = own.shape[0]
    square = jax.ShapeDtypeStruct((heads, WIDE, WIDE), bf16)
    vmem = pl.BlockSpec(memory_space=pltpu.VMEM)
    return pl.pallas_call(
        stage_kernel,
        in_specs=[pl.BlockSpec(memory_space=pltpu.SMEM), vmem, vmem, vmem],
        out_specs=[vmem, vmem, vmem],
        out_shape=[jax.ShapeDtypeStruct(own.shape, bf16), square, square],
        compiler_params=pltpu.CompilerParams(vmem_limit_bytes=40 * 1024 * 1024),
        name="stage",
    )(flag, own, other, prefix)


def finish_kernel(levels_ref, near_ref, rows_ref, weight_ref, *rest):
    *carry_refs, last_ref, prefix_ref, out_ref, weight_s = rest
    tokens = near_ref.shape[0]
    heads = near_ref.shape[1] // WIDE
    level = lax.rem(lax.broadcasted_iota(jnp.int32, (BLOCK, heads * LEVELS), 1), LEVELS)
    for b in range(tokens // BLOCK):
        part = slice(b * BLOCK, (b + 1) * BLOCK)
        weight_s[part, :] = jnp.where(level < levels_ref[b], weight_ref[part, :], 0.0)
    for h in range(heads):
        cols = slice(h * WIDE, (h + 1) * WIDE)
        parts = [ref[h] for ref in carry_refs]
        parts.append(mxu(prefix_ref[h], last_ref[h]).astype(bf16))
        far = mxu(rows_ref[:, cols], jnp.concatenate(parts, axis=1))
        total = near_ref[:, cols] * weight_s[:, h * LEVELS:h * LEVELS + 1]
        for i in range(len(parts)):
            at = h * LEVELS + 1 + i
            total = total + far[:, i * WIDE:(i + 1) * WIDE] * weight_s[:, at:at + 1]
        out_ref[:, cols] = total.astype(bf16)


def finish_call(levels, near, rows, weights, carries, last, prefix):
    vmem = pl.BlockSpec(memory_space=pltpu.VMEM)
    count = 3 + len(carries) + 2
    return pl.pallas_call(
        finish_kernel,
        in_specs=[pl.BlockSpec(memory_space=pltpu.SMEM)] + [vmem] * count,
        out_specs=vmem,
        out_shape=jax.ShapeDtypeStruct(near.shape, bf16),
        scratch_shapes=[pltpu.VMEM(weights.shape, f32)],
        compiler_params=pltpu.CompilerParams(vmem_limit_bytes=40 * 1024 * 1024),
        name="finish",
    )(levels, near, rows, weights, *carries, last, prefix)


def per_device(queries, key_rows, value_rows, log_decay, write_rate, level_weights, block_levels):
    heads = log_decay.shape[1]
    size = lax.axis_size("ctx")
    bits = size.bit_length() - 1
    position = lax.axis_index("ctx")
    run, near, rows = local_call(
        queries, key_rows, value_rows, rows_of(log_decay), rows_of(write_rate), 0, heads
    )
    prefix = jnp.broadcast_to(jnp.eye(WIDE, dtype=bf16), (heads, WIDE, WIDE))
    carries = []
    for bit in range(bits - 1):
        other = lax.ppermute(run, "ctx", [(i, i ^ 1 << bit) for i in range(size)])
        flag = (position >> bit & 1).astype(jnp.int32).reshape(1)
        run, carry, prefix = stage_call(flag, run, other, prefix)
        carries.append(carry)
    half = 1 << bits - 1
    last = lax.ppermute(run[..., :WIDE], "ctx", [(i, i + half) for i in range(half)])
    out = finish_call(block_levels, near, rows, level_weights, carries, last, prefix)
    return lax.all_to_all(out, "head", split_axis=0, concat_axis=1, tiled=True)


def solution(mesh):
    wide = P("ctx", "head")
    return jax.shard_map(
        per_device,
        mesh=mesh,
        in_specs=(wide, wide, wide, wide, wide, wide, P("ctx")),
        out_specs=P(("ctx", "head"), None),
        check_vma=False,
    )
```

```python
import jax
import jax.numpy as jnp
from jax import lax
from jax.sharding import PartitionSpec as P
from jax.experimental import pallas as pl
from jax.experimental.pallas import tpu as pltpu

BLOCK = 64
WIDE = 128
LEVELS = 5
SHARES = (8, 8)
f32 = jnp.float32
bf16 = jnp.bfloat16
MEG = 1024 * 1024
FINISH = 16
LOCAL = 62.25
GATHER = 8


def mxu(a, b):
    return lax.dot_general(a, b, (((1,), (0,)), ((), ())), preferred_element_type=f32)


def mxu_t(a, b):
    return lax.dot_general(a, b, (((1,), (1,)), ((), ())), preferred_element_type=f32)


def halves(x):
    hi = x.astype(bf16)
    return hi, (x - hi.astype(f32)).astype(bf16)


def together(live):
    while live:
        live = [g for g in live if next(g, g) is not g]


def repeat(count, body, unroll):
    while count % unroll:
        unroll -= 1

    def step(i, _):
        together([body(i * unroll + j) for j in range(unroll)])
        return 0

    lax.fori_loop(0, count // unroll, step, 0)


def split(heads, shares):
    counts = [heads * share // sum(shares) for share in shares]
    return [(sum(counts[:g]), n) for g, n in enumerate(counts)]


def aligned(index, size):
    return pl.ds(pl.multiple_of(index * size, size), size)


def left_half():
    return lax.broadcasted_iota(jnp.int32, (BLOCK, WIDE), 1) < BLOCK


def diagonal(x, left):
    zero = jnp.zeros_like(x)
    return jnp.concatenate([jnp.where(left, x, zero), jnp.where(left, zero, x)], axis=0)


def column(table, lane, at):
    picked = jnp.sum(jnp.where(lane == at, table, 0.0), axis=1, keepdims=True)
    return jnp.broadcast_to(picked, (BLOCK, WIDE))


def local_kernel(solve, span, heads, depth, levels_ref, *refs):
    first, count = span
    names = ["weight", "row", "col", "kn", "t", "q", "v"]
    if solve:
        names = ["weight", "ld", "wr", "k", "q", "v"]
    inputs, refs = dict(zip(names, refs)), refs[len(names):]
    run_ref, term_hbm, refs = refs[0], refs[1], refs[2:]
    if solve:
        row_s, colg_s, kn_hbm, t_hbm, refs = *refs[:4], refs[4:]
        ld_s, wr_s, k_s, low_s, inv_s, colb_s, key_sem, refs = *refs[:7], refs[7:]
    else:
        row_s, colg_s = inputs["row"], inputs["col"]
    (
        weight_s, q_s, v_s, kn_s, gram_s, scale_s, m_s, s_s, qt_s, near_s, p_s, term_s, copy_sem,
        keep_sem, step_sem,
    ) = refs
    tokens = q_s.shape[0]
    pairs = tokens // WIDE
    units = heads * pairs
    blocks = tokens // BLOCK
    lanes = 2 * units
    across = heads if solve else count
    mine = slice(first * WIDE, (first + count) * WIDE)

    loads = {
        "weight": (inputs["weight"], weight_s),
        "q": (inputs["q"].at[:, mine], q_s),
        "v": (inputs["v"].at[:, mine], v_s),
    }
    if solve:
        loads.update(ld=(inputs["ld"], ld_s), wr=(inputs["wr"], wr_s))
    else:
        loads["kn"] = (inputs["kn"].at[first:first + count], kn_s)
        for p in range(pairs):
            at = (p * heads + first) * BLOCK
            part = slice(p * count * BLOCK, (p + 1) * count * BLOCK)
            loads["t", p] = (inputs["t"].at[at:at + count * BLOCK], gram_s.at[part])
    loads = {
        name: pltpu.make_async_copy(x, y, copy_sem.at[i])
        for i, (name, (x, y)) in enumerate(loads.items())
    }
    if solve:
        quarter = k_s.shape[1] // 4

        def key_copy(i):
            part = aligned(i, quarter)
            return pltpu.make_async_copy(inputs["k"].at[:, part], k_s.at[:, part], key_sem.at[i])

        loads["ld"].start()
        loads["wr"].start()
        for i in range(4):
            key_copy(i).start()
    for name, c in loads.items():
        if name not in ("ld", "wr"):
            c.start()

    left = left_half()
    ri = lax.broadcasted_iota(jnp.int32, (WIDE, WIDE), 0)
    ci = lax.broadcasted_iota(jnp.int32, (WIDE, WIDE), 1)

    def inverses():
        tri = jnp.where((ri <= ci) & ((ri >= BLOCK) == (ci >= BLOCK)), 1.0, 0.0)
        def by_unit(x):
            return jnp.concatenate([x[:, p * WIDE:(p + 1) * WIDE] for p in range(pairs)], axis=0)

        loads["ld"].wait()
        loads["wr"].wait()
        grow = lax.dot_general(
            by_unit(ld_s[...]), tri, (((1,), (0,)), ((), ())),
            precision=lax.Precision.HIGHEST, preferred_element_type=f32,
        )
        row_s[...] = grow
        gcol = grow.T
        bcol = by_unit(wr_s[...]).T
        colg_s[...] = jnp.concatenate([gcol[:BLOCK], gcol[BLOCK:]], axis=1)
        colb_s[...] = jnp.concatenate([bcol[:BLOCK], bcol[BLOCK:]], axis=1)

        def keys(h):
            cols = aligned(h, WIDE)
            kf = k_s[:, cols].astype(f32)
            total = jnp.sum(kf * kf, axis=1, keepdims=True)
            yield
            kn = (kf * lax.rsqrt(total + 1e-6)).astype(bf16)
            kn_s[h] = kn
            grams = []
            for p in range(pairs):
                kp = kn[p * WIDE:(p + 1) * WIDE]
                grams.append(mxu_t(kp, kp))
            yield
            for p, g in enumerate(grams):
                gram_s[aligned(p * heads + h, BLOCK), :] = jnp.where(left, g[:BLOCK], g[BLOCK:])

        def key_group(i, _):
            key_copy(i).wait()
            together([keys(i * (heads // 4) + j) for j in range(heads // 4)])
            return 0

        lax.fori_loop(0, 4, key_group, 0)

        def to_lanes(i):
            a = gram_s[pl.ds(i, units, stride=BLOCK), :].T
            yield
            g = jnp.concatenate([a[:BLOCK], a[BLOCK:]], axis=1)
            gi = colg_s[pl.ds(i, 1), :]
            bi = colb_s[pl.ds(i, 1), :]
            e = jnp.exp(gi - colg_s[...])
            yield
            low_s[i] = g * (bi * e)
            inv_s[i] = jnp.zeros_like(g)

        repeat(BLOCK, to_lanes, 16)

        sub = lax.broadcasted_iota(jnp.int32, (8, lanes), 0)

        def solve(bi, _):
            i0 = bi * 8

            def columns(cb, _):
                c = aligned(cb, 8)

                def step(jb, acc):
                    acc = list(acc)
                    for jj in range(8):
                        j = jb * 8 + jj
                        t = inv_s[j, c, :]
                        for r in range(8):
                            acc[r] = acc[r] - low_s[i0 + r, pl.ds(j, 1), :] * t
                    return tuple(acc)

                on = cb == bi
                acc = tuple(jnp.where((sub == r) & on, 1.0, 0.0) for r in range(8))
                acc = list(lax.fori_loop(cb, bi, step, acc))
                for r in range(8):
                    inv_s[i0 + r, c, :] = acc[r]
                    for s in range(r + 1, 8):
                        acc[s] = acc[s] - low_s[i0 + s, pl.ds(i0 + r, 1), :] * acc[r]
                return 0

            lax.fori_loop(0, bi + 1, columns, 0)
            return 0

        lax.fori_loop(0, BLOCK // 8, solve, 0)

        def from_lanes(i):
            t = inv_s[i] * colb_s[...]
            a = jnp.concatenate([t[:, :units], t[:, units:]], axis=0).T
            yield
            gram_s[pl.ds(i, units, stride=BLOCK), :] = a

        repeat(BLOCK, from_lanes, 16)

    kept = []
    if solve:
        inverses()
        kept = [(kn_s, kn_hbm), (gram_s, t_hbm)]
        kept = [pltpu.make_async_copy(x, y, keep_sem.at[i]) for i, (x, y) in enumerate(kept)]
        for c in kept:
            c.start()
    for name, c in loads.items():
        if name not in ("ld", "wr", "weight"):
            c.wait()
    clane = lax.broadcasted_iota(jnp.int32, (BLOCK, lanes), 1)
    lane = lax.broadcasted_iota(jnp.int32, (BLOCK, WIDE), 1)
    row64 = lax.broadcasted_iota(jnp.int32, (BLOCK, WIDE), 0)
    keep = row64 >= jnp.where(left, lane, lane - BLOCK)
    eye = ri == ci

    def unit(i):
        p = i // count
        h = i - p * count
        u = p * heads + first + h
        grow = row_s[pl.ds(u, 1), :]
        gs = [column(colg_s[...], clane, u), column(colg_s[...], clane, u + units)]
        kn = kn_s[h, aligned(p, WIDE), :]
        v = v_s[aligned(p, WIDE), aligned(h, WIDE)]
        q = q_s[aligned(p, WIDE), aligned(h, WIDE)]
        qk = mxu_t(q, kn)
        t1 = gram_s[aligned(p * across + h, BLOCK), :]
        t2 = t1 * jnp.exp(grow)
        a_hi, a_lo = halves(diagonal(t1, left))
        b_hi, b_lo = halves(diagonal(t2, left))
        wv = mxu(jnp.concatenate([a_hi, a_lo], axis=1), jnp.concatenate([v, v], axis=0))
        wk = mxu(jnp.concatenate([b_hi, b_lo], axis=1), jnp.concatenate([kn, kn], axis=0))
        knt = kn.astype(f32).T.astype(bf16)
        decay = jnp.exp(jnp.where(keep, jnp.where(left, gs[0], gs[1]) - grow, -1e30))
        yield
        score = diagonal(jnp.where(left, qk[:BLOCK], qk[BLOCK:]) * decay, left).astype(bf16)
        w = jnp.concatenate([wv, wk], axis=1)
        kk = jnp.concatenate([knt, knt], axis=1)
        outs = []
        for half, g in enumerate(gs):
            end = g[BLOCK - 1:, :]
            tail = jnp.exp(end - g)
            part = w[half * BLOCK:(half + 1) * BLOCK] * jnp.concatenate([tail, tail], axis=1)
            hi, lo = halves(part)
            none = jnp.zeros_like(hi)
            stack = [hi, none, lo, none] if half == 0 else [none, hi, none, lo]
            outs.append((end, mxu(kk, jnp.concatenate(stack, axis=0))))
        ys = mxu(score, w.astype(bf16))
        yield
        for half, (end, y) in enumerate(outs):
            s_s[2 * p + half, h] = y[:, :WIDE]
            m = jnp.where(eye, jnp.exp(end), 0.0) - y[:, WIDE:]
            m_hi, m_lo = halves(m)
            m_s[2 * p + half, h] = jnp.concatenate([m_hi, m_lo], axis=1)
        near_s[i] = ys[:, :WIDE]
        eg = jnp.exp(jnp.concatenate(gs, axis=0))
        qt_s[i] = (eg * q.astype(f32) - ys[:, WIDE:]).astype(bf16)

    repeat(pairs * count, unit, 8)

    loads["weight"].wait()
    slots = weight_s.shape[0]
    level = lax.rem(lax.broadcasted_iota(jnp.int32, (BLOCK, slots), 1), LEVELS)
    weight = weight_s[...].T
    for b in range(blocks):
        toks = slice(b * BLOCK, (b + 1) * BLOCK)
        scale_s[toks, :] = jnp.where(level < levels_ref[b], weight[toks], 0.0)

    def term_copy(b):
        toks = aligned(b, BLOCK)
        return pltpu.make_async_copy(term_s.at[b], term_hbm.at[:, toks, :], step_sem.at[b])

    def write(b, h, near, rows):
        cols = pl.ds(h * WIDE, WIDE)
        scale = scale_s[aligned(b, BLOCK), :]
        for i in range(1 + depth):
            at = (first + h) * LEVELS + i
            term_s[b, i, :, cols] = ((rows if i else near) * scale[:, at:at + 1]).astype(bf16)

    for h in range(count):
        m = m_s[0, h]
        p_s[h, :, :WIDE] = s_s[0, h]
        p_s[h, :, WIDE:] = m[:, :WIDE].astype(f32) + m[:, WIDE:].astype(f32)
        write(0, h, near_s[h, :BLOCK, :], qt_s[h, :BLOCK, :].astype(f32))
    term_copy(0).start()

    def scan(b, _):
        half = aligned(b % 2, BLOCK)

        def advance(h):
            i = (b // 2) * count + h
            p_hi, p_lo = halves(p_s[h])
            m = m_s[b, h]
            n = mxu(
                jnp.concatenate([m, m[:, :WIDE]], axis=1),
                jnp.concatenate([p_hi, p_hi, p_lo], axis=0),
            )
            o = mxu(qt_s[i, half, :], p_hi)
            yield
            p_s[h, :, :WIDE] = n[:, :WIDE] + s_s[b, h]
            p_s[h, :, WIDE:] = n[:, WIDE:]
            write(b, h, near_s[i, half, :] + o[:, :WIDE], o[:, WIDE:])

        for h in range(0, count, 4):
            together([advance(h + j) for j in range(min(4, count - h))])
        term_copy(b).start()
        return 0

    lax.fori_loop(1, blocks, scan, 0)
    for h in range(count):
        run_ref[h] = p_s[h].astype(bf16)
    for c in kept:
        c.wait()
    for b in range(blocks):
        term_copy(b).wait()


def local_call(span, heads, depth, levels, weights, solved, inputs, q, v, after):
    tokens = q.shape[0]
    first, count = span
    pairs = tokens // WIDE
    units = heads * pairs
    blocks = tokens // BLOCK
    solve = solved is None
    smem = pl.BlockSpec(memory_space=pltpu.SMEM)
    vmem = pl.BlockSpec(memory_space=pltpu.VMEM)
    hbm = pl.BlockSpec(memory_space=pltpu.HBM)
    after, spaces = waits(after)
    out_specs = [vmem, hbm]
    out_shape = [
        jax.ShapeDtypeStruct((count, WIDE, 2 * WIDE), bf16),
        jax.ShapeDtypeStruct((1 + depth, tokens, count * WIDE), bf16),
    ]
    scratch = []
    if solve:
        operands = [weights, *inputs, q, v]
        in_specs = [hbm] * 6
        out_specs += [vmem, vmem, hbm, hbm]
        out_shape += [
            jax.ShapeDtypeStruct((units, WIDE), f32),
            jax.ShapeDtypeStruct((BLOCK, 2 * units), f32),
            jax.ShapeDtypeStruct((heads, tokens, WIDE), bf16),
            jax.ShapeDtypeStruct((units * BLOCK, WIDE), f32),
        ]
        scratch = [
            pltpu.VMEM(inputs[0].shape, f32),
            pltpu.VMEM(inputs[1].shape, f32),
            pltpu.VMEM(inputs[2].shape, bf16),
            pltpu.VMEM((BLOCK, BLOCK, 2 * units), f32),
            pltpu.VMEM((BLOCK, BLOCK, 2 * units), f32),
            pltpu.VMEM((BLOCK, 2 * units), f32),
            pltpu.SemaphoreType.DMA((4,)),
        ]
    else:
        operands = [weights, *solved, q, v]
        in_specs = [hbm, vmem, vmem, hbm, hbm, hbm, hbm]
    across = heads if solve else count

    def kernel(*refs):
        used = 1 + len(operands)
        local_kernel(solve, span, heads, depth, *refs[:used], *refs[used + len(after):])

    return pl.pallas_call(
        kernel,
        in_specs=[smem] + in_specs + spaces,
        out_specs=out_specs,
        out_shape=out_shape,
        scratch_shapes=scratch
        + [
            pltpu.VMEM(weights.shape, f32),
            pltpu.VMEM((tokens, count * WIDE), bf16),
            pltpu.VMEM((tokens, count * WIDE), bf16),
            pltpu.VMEM((across, tokens, WIDE), bf16),
            pltpu.VMEM((across * pairs * BLOCK, WIDE), f32),
            pltpu.VMEM((tokens, weights.shape[0]), f32),
            pltpu.VMEM((blocks, count, WIDE, 2 * WIDE), bf16),
            pltpu.VMEM((blocks, count, WIDE, WIDE), f32),
            pltpu.VMEM((pairs * count, WIDE, WIDE), bf16),
            pltpu.VMEM((pairs * count, WIDE, WIDE), f32),
            pltpu.VMEM((count, WIDE, 2 * WIDE), f32),
            pltpu.VMEM((blocks, 1 + depth, BLOCK, count * WIDE), bf16),
            pltpu.SemaphoreType.DMA((5 + pairs,)),
            pltpu.SemaphoreType.DMA((2,)),
            pltpu.SemaphoreType.DMA((blocks,)),
        ],
        compiler_params=pltpu.CompilerParams(vmem_limit_bytes=int(LOCAL * MEG)),
        name="local",
    )(levels, *operands, *after)


def waits(after):
    return [x for x, _ in after], [pl.BlockSpec(memory_space=space) for _, space in after]


def pair_kernel(flag_ref, own_ref, other_ref, *rest):
    s_ref, m_ref = rest[-2:]
    heads = own_ref.shape[0]
    upper = flag_ref[0] == 1

    def head(h):
        own = own_ref[h]
        other = other_ref[h]
        late = jnp.where(upper, own, other)
        early = jnp.where(upper, other, own)
        both = mxu(late[:, WIDE:], early)
        yield
        s_ref[h] = (both[:, :WIDE] + late[:, :WIDE].astype(f32)).astype(bf16)
        m_ref[h] = both[:, WIDE:].astype(bf16)

    together([head(h) for h in range(heads)])


def pair_call(flag, own, other, after):
    square = jax.ShapeDtypeStruct((own.shape[0], WIDE, WIDE), bf16)
    vmem = pl.BlockSpec(memory_space=pltpu.VMEM)
    after, spaces = waits(after)
    return pl.pallas_call(
        pair_kernel,
        in_specs=[pl.BlockSpec(memory_space=pltpu.SMEM), vmem, vmem]
        + spaces,
        out_specs=[vmem, vmem],
        out_shape=[square, square],
        compiler_params=pltpu.CompilerParams(vmem_limit_bytes=8 * MEG),
        name="pair",
    )(flag, own, other, *after)


def hop_kernel(m_ref, *refs):
    *entry_refs, out_ref = refs

    def head(h):
        entry = entry_refs[1][h]
        for ref in entry_refs[2:]:
            entry = (entry.astype(f32) + ref[h].astype(f32)).astype(bf16)
        o = mxu(m_ref[h], entry)
        yield
        if entry_refs[0] is not None:
            o = o + entry_refs[0][h].astype(f32)
        out_ref[h] = o.astype(bf16)

    together([head(h) for h in range(m_ref.shape[0])])


def hop_call(m, s, entries, after):
    vmem = pl.BlockSpec(memory_space=pltpu.VMEM)
    operands = ([] if s is None else [s]) + entries

    after, spaces = waits(after)

    def kernel(m_ref, *refs):
        used = refs[:len(operands)] + refs[-1:]
        hop_kernel(m_ref, *(used if s is not None else (None,) + used))

    return pl.pallas_call(
        kernel,
        in_specs=[vmem] * (1 + len(operands)) + spaces,
        out_specs=vmem,
        out_shape=jax.ShapeDtypeStruct(m.shape, bf16),
        compiler_params=pltpu.CompilerParams(vmem_limit_bytes=8 * MEG),
        name="hop",
    )(m, *operands, *after)


def finish_kernel(size, shape, here_ref, term_ref, other_ref, *refs):
    entries, at = [], 0
    for count in shape:
        entries.append(refs[at:at + count])
        at += count
    outs = refs[at:at + size]
    depth, tokens, width = term_ref.shape
    chunk = tokens // size
    heads = width // WIDE
    here = here_ref[0]
    position = here_ref[1]
    zero = jnp.zeros((WIDE, WIDE), bf16)
    odd = (position & 1) == 1
    pair = position >> 1
    carries = []
    for h in range(heads):
        came = []
        for m, options in enumerate(entries):
            entry = zero
            for j, ref in enumerate(options):
                mine = ((pair >> m) & 1 == 1) & ((pair & ((1 << m) - 1)) == j)
                entry = jnp.where(mine, ref[h], entry)
            came.append(entry)
        wide = jnp.concatenate(came, axis=1)
        ahead = mxu(other_ref[h, :, WIDE:], wide).astype(bf16)
        carries.append(jnp.concatenate(
            [jnp.where(odd, other_ref[h, :, :WIDE], zero)]
            + [
                jnp.where(odd, ahead[:, m * WIDE:(m + 1) * WIDE], x) for m, x in enumerate(came)
            ],
            axis=0,
        ))
    for d in range(size):
        toks = aligned(here ^ d, chunk)

        def head(h):
            part = slice(h * WIDE, (h + 1) * WIDE)
            far = jnp.concatenate([term_ref[i, toks, part] for i in range(1, depth)], axis=1)
            total = mxu(far, carries[h])
            yield
            outs[d][:, part] = (total + term_ref[0, toks, part].astype(f32)).astype(bf16)

        together([head(h) for h in range(heads)])


def finish_call(size, here, terms, other, entries, after):
    depth, tokens, width = terms.shape
    smem = pl.BlockSpec(memory_space=pltpu.SMEM)
    vmem = pl.BlockSpec(memory_space=pltpu.VMEM)
    shape = [len(e) for e in entries]
    flat = [x for e in entries for x in e]
    after, spaces = waits(after)

    def kernel(*refs):
        used = 3 + len(flat)
        finish_kernel(size, shape, *refs[:used], *refs[used + len(after):])

    return pl.pallas_call(
        kernel,
        in_specs=[smem] + [vmem] * (2 + len(flat)) + spaces,
        out_specs=[vmem] * size,
        out_shape=[jax.ShapeDtypeStruct((tokens // size, width), bf16)] * size,
        compiler_params=pltpu.CompilerParams(vmem_limit_bytes=FINISH * MEG),
        name="finish",
    )(here, terms, other, *flat, *after)


def gather_kernel(first, heads, size, place_ref, *refs):
    parts, (out_ref, sems) = refs[:size], refs[-2:]
    here = place_ref[0]
    copies = []
    for d, ref in enumerate(parts):
        col = pl.multiple_of(((here ^ d) * heads + first) * WIDE, WIDE)
        where = out_ref.at[:, pl.ds(col, ref.shape[1])]
        copies.append(pltpu.make_async_copy(ref, where, sems.at[d]))
        copies[-1].start()
    for c in copies:
        c.wait()


def gather_call(first, heads, place, parts, before, after):
    size = len(parts)
    vmem = pl.BlockSpec(memory_space=pltpu.VMEM)
    hbm = pl.BlockSpec(memory_space=pltpu.HBM)
    after, spaces = waits(after)
    kept = [] if before is None else [before]

    def kernel(*refs):
        gather_kernel(first, heads, size, *refs)

    return pl.pallas_call(
        kernel,
        in_specs=[pl.BlockSpec(memory_space=pltpu.SMEM)] + [vmem] * size + [hbm] * len(kept)
        + spaces,
        out_specs=hbm,
        out_shape=jax.ShapeDtypeStruct((parts[0].shape[0], heads * size * WIDE), bf16),
        input_output_aliases={1 + size: 0} if kept else {},
        scratch_shapes=[pltpu.SemaphoreType.DMA((size,))],
        compiler_params=pltpu.CompilerParams(vmem_limit_bytes=GATHER * MEG),
        name="gather",
    )(place, *parts, *kept, *after)


ORDER = ("l0", "l1", "p0", "h01", "p1", "h02", "h11", "f0", "h12", "f1", "g0", "g1")


def order(groups, steps):
    names = dict(l="local", p="pair", h="hop", f="finish", g="gather")
    if steps == 3:
        return [(names[x[0]], int(x[1]), int(x[2:] or 0)) for x in ORDER]
    out = [("local", g, 0) for g in range(groups)] + [("pair", g, 0) for g in range(groups)]
    out += [("hop", g, step) for step in range(1, steps) for g in range(groups)]
    out += [("finish", g, 0) for g in range(groups)]
    return out + [("gather", g, 0) for g in range(groups)]


def per_device(queries, key_rows, value_rows, log_decay, write_rate, level_weights, block_levels):
    size = lax.axis_size("ctx")
    bits = size.bit_length() - 1
    width = lax.axis_size("head")
    position = lax.axis_index("ctx").astype(jnp.int32)
    place = lax.axis_index("head").astype(jnp.int32)
    here = jnp.stack([place, position])
    flag = (position & 1).reshape(1)
    heads = log_decay.shape[1]
    groups = split(heads, SHARES)
    pairs = size // 2
    steps = [(m, j) for m in range(pairs.bit_length() - 1) for j in range(1 << m)]

    def swap(low, array):
        to = list(range(pairs))
        for p in low:
            to[p], to[p + 1] = p + 1, p
        return lax.ppermute(array, "ctx", [(i, 2 * to[i >> 1] + (i & 1)) for i in range(size)])

    runs, others, terms, states, solved = {}, {}, {}, {}, []
    entries = [[] for _ in groups]
    pieces = {}
    after = []

    def local(g):
        runs[g], terms[g], *kept = local_call(
            groups[g], heads, bits, block_levels, level_weights.T, solved[0] if solved else None,
            [log_decay.T, write_rate.T, key_rows], queries, value_rows, after,
        )
        if kept:
            solved.append(kept)
        others[g] = lax.ppermute(runs[g], "ctx", [(i, i ^ 1) for i in range(size)])
        return terms[g], pltpu.HBM

    def pair(g):
        states[g] = pair_call(flag, runs[g], others[g], after)
        return states[g][1], pltpu.VMEM

    def hop(g, step):
        m, j = steps[step]
        s, t = states[g]
        if j:
            sent = hop_call(t, None, [entries[g][m][j - 1]], after)
        elif m:
            sent = hop_call(t, s, [e[-1] for e in entries[g]], after)
        else:
            sent = s
        if j == 0:
            entries[g].append([])
        low = [p for p in range(pairs) if p % (2 << m) == (1 << m) + j - 1]
        entries[g][m].append(swap(low, sent))
        return sent, pltpu.VMEM

    def finish(g):
        outs = finish_call(width, here, terms[g], others[g], entries[g], after)
        for d in range(width):
            pairing = [(i, i ^ d) for i in range(width)]
            pieces[g, d] = outs[d] if d == 0 else lax.ppermute(outs[d], "head", pairing)
        return outs[0], pltpu.VMEM

    def gather(g, out):
        parts = [pieces[g, d] for d in range(width)]
        return gather_call(groups[g][0], heads, place.reshape(1), parts, out, after)

    out = None
    for name, g, step in order(len(groups), len(steps)):
        if name == "local":
            token = local(g)
        elif name == "pair":
            token = pair(g)
            hop(g, 0)
        elif name == "hop":
            token = hop(g, step)
        elif name == "finish":
            token = finish(g)
        else:
            out = gather(g, out)
            token = out, pltpu.HBM
        after = [token]
    return out


def solution(mesh):
    wide = P("ctx", "head")
    return jax.shard_map(
        per_device,
        mesh=mesh,
        in_specs=(wide, wide, wide, wide, wide, wide, P("ctx")),
        out_specs=P(("ctx", "head"), None),
        check_vma=False,
    )
```

```python
import jax
import jax.numpy as jnp
from jax import lax
from jax.sharding import PartitionSpec as P
from jax.experimental import pallas as pl
from jax.experimental.pallas import tpu as pltpu

BLOCK = 64
WIDE = 128
LEVELS = 5
SHARES = (8, 8)
f32 = jnp.float32
bf16 = jnp.bfloat16
MEG = 1024 * 1024
FINISH = 16
LOCAL = 62.25
PARTS = 1
SIDE = 4
GATHER = 8


def mxu(a, b):
    return lax.dot_general(a, b, (((1,), (0,)), ((), ())), preferred_element_type=f32)


def mxu_t(a, b):
    return lax.dot_general(a, b, (((1,), (1,)), ((), ())), preferred_element_type=f32)


def halves(x):
    hi = x.astype(bf16)
    return hi, (x - hi.astype(f32)).astype(bf16)


def together(live):
    while live:
        live = [g for g in live if next(g, g) is not g]


def repeat(count, body, unroll):
    while count % unroll:
        unroll -= 1

    def step(i, _):
        together([body(i * unroll + j) for j in range(unroll)])
        return 0

    lax.fori_loop(0, count // unroll, step, 0)


def split(heads, shares):
    counts = [heads * share // sum(shares) for share in shares]
    counts[-1] = heads - sum(counts[:-1])
    return [(sum(counts[:g]), n) for g, n in enumerate(counts)]


def aligned(index, size):
    return pl.ds(pl.multiple_of(index * size, size), size)


def left_half():
    return lax.broadcasted_iota(jnp.int32, (BLOCK, WIDE), 1) < BLOCK


def diagonal(x, left):
    zero = jnp.zeros_like(x)
    return jnp.concatenate([jnp.where(left, x, zero), jnp.where(left, zero, x)], axis=0)


def column(table, lane, at):
    picked = jnp.sum(jnp.where(lane == at, table, 0.0), axis=1, keepdims=True)
    return jnp.broadcast_to(picked, (BLOCK, WIDE))


def local_kernel(solve, span, heads, depth, levels_ref, *refs):
    first, count = span
    names = ["weight", "row", "col", "kn", "t", "q", "v"]
    if solve:
        names = ["weight", "ld", "wr", "k", "q", "v"]
    inputs, refs = dict(zip(names, refs)), refs[len(names):]
    run_ref, term_hbm, mark_ref, refs = *refs[:3], refs[3:]
    mark_ref[...] = jnp.zeros_like(mark_ref)
    if solve:
        row_s, colg_s, kn_hbm, t_hbm, refs = *refs[:4], refs[4:]
        ld_s, wr_s, k_s, low_s, inv_s, colb_s, key_sem, refs = *refs[:7], refs[7:]
    else:
        row_s, colg_s = inputs["row"], inputs["col"]
    (
        weight_s, q_s, v_s, kn_s, gram_s, scale_s, m_s, fall_s, s_s, qt_s, near_s, p_s, term_s, copy_sem,
        pair_sem, keep_sem, step_sem,
    ) = refs
    tokens = q_s.shape[0]
    pairs = tokens // WIDE
    units = heads * pairs
    blocks = tokens // BLOCK
    lanes = 2 * units
    across = heads if solve else count
    mine = slice(first * WIDE, (first + count) * WIDE)

    loads = {"weight": (inputs["weight"], weight_s)}
    if solve:
        loads.update(ld=(inputs["ld"], ld_s), wr=(inputs["wr"], wr_s))

    def pair_copies(p):
        toks = aligned(p, WIDE)
        copies = [
            (inputs["q"].at[toks, mine], q_s.at[toks, :]),
            (inputs["v"].at[toks, mine], v_s.at[toks, :]),
        ]
        if not solve:
            size = count * BLOCK
            at = pl.ds(pl.multiple_of((p * heads + first) * BLOCK, BLOCK), size)
            copies += [
                (inputs["kn"].at[first:first + count, toks, :], kn_s.at[:, toks, :]),
                (inputs["t"].at[at, :], gram_s.at[aligned(p, size), :]),
            ]
        return [
            pltpu.make_async_copy(x, y, pair_sem.at[p, i]) for i, (x, y) in enumerate(copies)
        ]

    if solve:
        for i, name in enumerate(("q", "v")):
            loads[name] = (inputs[name].at[:, mine], (q_s, v_s)[i])

    loads = {
        name: pltpu.make_async_copy(x, y, copy_sem.at[i])
        for i, (name, (x, y)) in enumerate(loads.items())
    }
    if solve:
        quarter = k_s.shape[1] // 4

        def key_copy(i):
            part = aligned(i, quarter)
            return pltpu.make_async_copy(inputs["k"].at[:, part], k_s.at[:, part], key_sem.at[i])

        loads["ld"].start()
        loads["wr"].start()
        for i in range(4):
            key_copy(i).start()
    if not solve:
        for p in range(pairs):
            for c in pair_copies(p):
                c.start()
    for name, c in loads.items():
        if name not in ("ld", "wr"):
            c.start()

    left = left_half()
    ri = lax.broadcasted_iota(jnp.int32, (WIDE, WIDE), 0)
    ci = lax.broadcasted_iota(jnp.int32, (WIDE, WIDE), 1)

    def inverses():
        tri = jnp.where((ri <= ci) & ((ri >= BLOCK) == (ci >= BLOCK)), 1.0, 0.0)
        def by_unit(x):
            return jnp.concatenate([x[:, p * WIDE:(p + 1) * WIDE] for p in range(pairs)], axis=0)

        loads["ld"].wait()
        loads["wr"].wait()
        grow = lax.dot_general(
            by_unit(ld_s[...]), tri, (((1,), (0,)), ((), ())),
            precision=lax.Precision.HIGHEST, preferred_element_type=f32,
        )
        row_s[...] = grow
        gcol = grow.T
        bcol = by_unit(wr_s[...]).T
        colg_s[...] = jnp.concatenate([gcol[:BLOCK], gcol[BLOCK:]], axis=1)
        colb_s[...] = jnp.concatenate([bcol[:BLOCK], bcol[BLOCK:]], axis=1)

        def keys(h):
            cols = aligned(h, WIDE)
            kf = k_s[:, cols].astype(f32)
            total = jnp.sum(kf * kf, axis=1, keepdims=True)
            yield
            kn = (kf * lax.rsqrt(total + 1e-6)).astype(bf16)
            kn_s[h] = kn
            grams = []
            for p in range(pairs):
                kp = kn[p * WIDE:(p + 1) * WIDE]
                grams.append(mxu_t(kp, kp))
            yield
            for p, g in enumerate(grams):
                gram_s[aligned(p * heads + h, BLOCK), :] = jnp.where(left, g[:BLOCK], g[BLOCK:])

        def key_group(i, _):
            key_copy(i).wait()
            together([keys(i * (heads // 4) + j) for j in range(heads // 4)])
            return 0

        lax.fori_loop(0, 4, key_group, 0)

        def to_lanes(i):
            a = gram_s[pl.ds(i, units, stride=BLOCK), :].T
            yield
            g = jnp.concatenate([a[:BLOCK], a[BLOCK:]], axis=1)
            gi = colg_s[pl.ds(i, 1), :]
            bi = colb_s[pl.ds(i, 1), :]
            e = jnp.exp(gi - colg_s[...])
            yield
            low_s[i] = g * (bi * e)
            inv_s[i] = jnp.zeros_like(g)

        repeat(BLOCK, to_lanes, 16)

        sub = lax.broadcasted_iota(jnp.int32, (8, lanes), 0)

        def solve(bi, _):
            i0 = bi * 8

            def columns(cb, _):
                c = aligned(cb, 8)

                def step(jb, acc):
                    acc = list(acc)
                    for jj in range(8):
                        j = jb * 8 + jj
                        t = inv_s[j, c, :]
                        for r in range(8):
                            acc[r] = acc[r] - low_s[i0 + r, pl.ds(j, 1), :] * t
                    return tuple(acc)

                on = cb == bi
                acc = tuple(jnp.where((sub == r) & on, 1.0, 0.0) for r in range(8))
                acc = list(lax.fori_loop(cb, bi, step, acc))
                for r in range(8):
                    inv_s[i0 + r, c, :] = acc[r]
                    for s in range(r + 1, 8):
                        acc[s] = acc[s] - low_s[i0 + s, pl.ds(i0 + r, 1), :] * acc[r]
                return 0

            lax.fori_loop(0, bi + 1, columns, 0)
            return 0

        lax.fori_loop(0, BLOCK // 8, solve, 0)

        def from_lanes(i):
            t = inv_s[i] * colb_s[...]
            a = jnp.concatenate([t[:, :units], t[:, units:]], axis=0).T
            yield
            gram_s[pl.ds(i, units, stride=BLOCK), :] = a

        repeat(BLOCK, from_lanes, 16)

    kept = []
    if solve:
        inverses()
        kept = [(kn_s, kn_hbm), (gram_s, t_hbm)]
        kept = [pltpu.make_async_copy(x, y, keep_sem.at[i]) for i, (x, y) in enumerate(kept)]
        for c in kept:
            c.start()
    clane = lax.broadcasted_iota(jnp.int32, (BLOCK, lanes), 1)
    lane = lax.broadcasted_iota(jnp.int32, (BLOCK, WIDE), 1)
    row64 = lax.broadcasted_iota(jnp.int32, (BLOCK, WIDE), 0)
    keep = row64 >= jnp.where(left, lane, lane - BLOCK)
    eye = ri == ci

    def unit(p, h):
        i = p * count + h
        u = p * heads + first + h
        grow = row_s[pl.ds(u, 1), :]
        gs = [column(colg_s[...], clane, u), column(colg_s[...], clane, u + units)]
        kn = kn_s[h, aligned(p, WIDE), :]
        v = v_s[aligned(p, WIDE), aligned(h, WIDE)]
        q = q_s[aligned(p, WIDE), aligned(h, WIDE)]
        qk = mxu_t(q, kn)
        t1 = gram_s[aligned(p * across + h, BLOCK), :]
        t2 = t1 * jnp.exp(grow)
        a_hi, a_lo = halves(diagonal(t1, left))
        b_hi, b_lo = halves(diagonal(t2, left))
        wv = mxu(jnp.concatenate([a_hi, a_lo], axis=1), jnp.concatenate([v, v], axis=0))
        wk = mxu(jnp.concatenate([b_hi, b_lo], axis=1), jnp.concatenate([kn, kn], axis=0))
        knt = kn.astype(f32).T.astype(bf16)
        decay = jnp.exp(jnp.where(keep, jnp.where(left, gs[0], gs[1]) - grow, -1e30))
        yield
        score = diagonal(jnp.where(left, qk[:BLOCK], qk[BLOCK:]) * decay, left).astype(bf16)
        w = jnp.concatenate([wv, wk], axis=1)
        kk = jnp.concatenate([knt, knt], axis=1)
        outs = []
        for half, g in enumerate(gs):
            end = g[BLOCK - 1:, :]
            tail = jnp.exp(end - g)
            part = w[half * BLOCK:(half + 1) * BLOCK] * jnp.concatenate([tail, tail], axis=1)
            hi, lo = halves(part)
            none = jnp.zeros_like(hi)
            stack = [hi, none, lo, none] if half == 0 else [none, hi, none, lo]
            outs.append((end, mxu(kk, jnp.concatenate(stack, axis=0))))
        ys = mxu(score, w.astype(bf16))
        yield
        for half, (end, y) in enumerate(outs):
            s_s[2 * p + half, h] = y[:, :WIDE]
            m_s[2 * p + half, h] = y[:, WIDE:].astype(bf16)
            fall_s[2 * p + half, pl.ds(h, 1), :] = jnp.exp(end)
        near_s[i] = ys[:, :WIDE]
        eg = jnp.exp(jnp.concatenate(gs, axis=0))
        qt_s[i] = (eg * q.astype(f32) - ys[:, WIDE:]).astype(bf16)

    if solve:
        loads["q"].wait()
        loads["v"].wait()

    def pair_units(p, _):
        if not solve:
            for c in pair_copies(p):
                c.wait()
        repeat(count, lambda h: unit(p, h), 8)
        return 0

    lax.fori_loop(0, pairs, pair_units, 0)

    loads["weight"].wait()
    slots = weight_s.shape[0]
    level = lax.rem(lax.broadcasted_iota(jnp.int32, (BLOCK, slots), 1), LEVELS)
    weight = weight_s[...].T
    for b in range(blocks):
        toks = slice(b * BLOCK, (b + 1) * BLOCK)
        scale_s[toks, :] = jnp.where(level < levels_ref[b], weight[toks], 0.0)

    def term_copy(b):
        toks = aligned(b, BLOCK)
        return pltpu.make_async_copy(term_s.at[b], term_hbm.at[:, toks, :], step_sem.at[b])

    def write(b, h, near, rows):
        cols = pl.ds(h * WIDE, WIDE)
        scale = scale_s[aligned(b, BLOCK), :]
        for i in range(1 + depth):
            at = (first + h) * LEVELS + i
            term_s[b, i, :, cols] = ((rows if i else near) * scale[:, at:at + 1]).astype(bf16)

    for h in range(count):
        p_s[h, :, :WIDE] = s_s[0, h]
        p_s[h, :, WIDE:] = jnp.where(eye, fall_s[0, h:h + 1, :], 0.0) - m_s[0, h].astype(f32)
        write(0, h, near_s[h, :BLOCK, :], qt_s[h, :BLOCK, :].astype(f32))
    term_copy(0).start()

    def scan(b, _):
        half = aligned(b % 2, BLOCK)

        def advance(h):
            i = (b // 2) * count + h
            both = mxu(
                jnp.concatenate([m_s[b, h], qt_s[i, half, :]], axis=0), p_s[h].astype(bf16)
            )
            yield
            fall = fall_s[b, h:h + 1, :]
            n, o = both[:WIDE], both[WIDE:]
            p_s[h, :, :WIDE] = fall * p_s[h, :, :WIDE] + s_s[b, h] - n[:, :WIDE]
            p_s[h, :, WIDE:] = fall * p_s[h, :, WIDE:] - n[:, WIDE:]
            write(b, h, near_s[i, half, :] + o[:, :WIDE], o[:, WIDE:])

        for h in range(0, count, SIDE):
            together([advance(h + j) for j in range(min(SIDE, count - h))])
        term_copy(b).start()
        return 0

    lax.fori_loop(1, blocks, scan, 0)
    for h in range(count):
        run_ref[h] = p_s[h].astype(bf16)
    for c in kept:
        c.wait()
    for b in range(blocks):
        term_copy(b).wait()


def local_call(span, heads, depth, levels, weights, solved, inputs, q, v, after):
    tokens = q.shape[0]
    first, count = span
    pairs = tokens // WIDE
    units = heads * pairs
    blocks = tokens // BLOCK
    solve = solved is None
    smem = pl.BlockSpec(memory_space=pltpu.SMEM)
    vmem = pl.BlockSpec(memory_space=pltpu.VMEM)
    hbm = pl.BlockSpec(memory_space=pltpu.HBM)
    after, spaces = waits(after)
    out_specs = [vmem, hbm, vmem]
    out_shape = [
        jax.ShapeDtypeStruct((count, WIDE, 2 * WIDE), bf16),
        jax.ShapeDtypeStruct((1 + depth, tokens, count * WIDE), bf16),
        jax.ShapeDtypeStruct((8, WIDE), f32),
    ]
    scratch = []
    if solve:
        operands = [weights, *inputs, q, v]
        in_specs = [hbm] * 6
        out_specs += [vmem, vmem, hbm, hbm]
        out_shape += [
            jax.ShapeDtypeStruct((units, WIDE), f32),
            jax.ShapeDtypeStruct((BLOCK, 2 * units), f32),
            jax.ShapeDtypeStruct((heads, tokens, WIDE), bf16),
            jax.ShapeDtypeStruct((units * BLOCK, WIDE), f32),
        ]
        scratch = [
            pltpu.VMEM(inputs[0].shape, f32),
            pltpu.VMEM(inputs[1].shape, f32),
            pltpu.VMEM(inputs[2].shape, bf16),
            pltpu.VMEM((BLOCK, BLOCK, 2 * units), f32),
            pltpu.VMEM((BLOCK, BLOCK, 2 * units), f32),
            pltpu.VMEM((BLOCK, 2 * units), f32),
            pltpu.SemaphoreType.DMA((4,)),
        ]
    else:
        operands = [weights, *solved, q, v]
        in_specs = [hbm, vmem, vmem, hbm, hbm, hbm, hbm]
    across = heads if solve else count

    def kernel(*refs):
        used = 1 + len(operands)
        local_kernel(solve, span, heads, depth, *refs[:used], *refs[used + len(after):])

    return pl.pallas_call(
        kernel,
        in_specs=[smem] + in_specs + spaces,
        out_specs=out_specs,
        out_shape=out_shape,
        scratch_shapes=scratch
        + [
            pltpu.VMEM(weights.shape, f32),
            pltpu.VMEM((tokens, count * WIDE), bf16),
            pltpu.VMEM((tokens, count * WIDE), bf16),
            pltpu.VMEM((across, tokens, WIDE), bf16),
            pltpu.VMEM((across * pairs * BLOCK, WIDE), f32),
            pltpu.VMEM((tokens, weights.shape[0]), f32),
            pltpu.VMEM((blocks, count, WIDE, WIDE), bf16),
            pltpu.VMEM((blocks, count, WIDE), f32),
            pltpu.VMEM((blocks, count, WIDE, WIDE), f32),
            pltpu.VMEM((pairs * count, WIDE, WIDE), bf16),
            pltpu.VMEM((pairs * count, WIDE, WIDE), f32),
            pltpu.VMEM((count, WIDE, 2 * WIDE), f32),
            pltpu.VMEM((blocks, 1 + depth, BLOCK, count * WIDE), bf16),
            pltpu.SemaphoreType.DMA((5,)),
            pltpu.SemaphoreType.DMA((pairs, 4)),
            pltpu.SemaphoreType.DMA((2,)),
            pltpu.SemaphoreType.DMA((blocks,)),
        ],
        compiler_params=pltpu.CompilerParams(vmem_limit_bytes=int(LOCAL * MEG)),
        name="local",
    )(levels, *operands, *after)


def waits(after):
    return [x for x, _ in after], [pl.BlockSpec(memory_space=space) for _, space in after]


def pair_kernel(flag_ref, own_ref, other_ref, *rest):
    s_ref, m_ref = rest[-2:]
    heads = own_ref.shape[0]
    upper = flag_ref[0] == 1

    def head(h):
        own = own_ref[h]
        other = other_ref[h]
        late = jnp.where(upper, own, other)
        early = jnp.where(upper, other, own)
        both = mxu(late[:, WIDE:], early)
        yield
        s_ref[h] = (both[:, :WIDE] + late[:, :WIDE].astype(f32)).astype(bf16)
        m_ref[h] = both[:, WIDE:].astype(bf16)

    together([head(h) for h in range(heads)])


def pair_call(flag, own, other, after):
    square = jax.ShapeDtypeStruct((own.shape[0], WIDE, WIDE), bf16)
    vmem = pl.BlockSpec(memory_space=pltpu.VMEM)
    after, spaces = waits(after)
    return pl.pallas_call(
        pair_kernel,
        in_specs=[pl.BlockSpec(memory_space=pltpu.SMEM), vmem, vmem]
        + spaces,
        out_specs=[vmem, vmem],
        out_shape=[square, square],
        compiler_params=pltpu.CompilerParams(vmem_limit_bytes=8 * MEG),
        name="pair",
    )(flag, own, other, *after)


def hop_kernel(m_ref, *refs):
    *entry_refs, out_ref = refs

    def head(h):
        entry = entry_refs[1][h]
        for ref in entry_refs[2:]:
            entry = (entry.astype(f32) + ref[h].astype(f32)).astype(bf16)
        o = mxu(m_ref[h], entry)
        yield
        if entry_refs[0] is not None:
            o = o + entry_refs[0][h].astype(f32)
        out_ref[h] = o.astype(bf16)

    together([head(h) for h in range(m_ref.shape[0])])


def hop_call(m, s, entries, after):
    vmem = pl.BlockSpec(memory_space=pltpu.VMEM)
    operands = ([] if s is None else [s]) + entries

    after, spaces = waits(after)

    def kernel(m_ref, *refs):
        used = refs[:len(operands)] + refs[-1:]
        hop_kernel(m_ref, *(used if s is not None else (None,) + used))

    return pl.pallas_call(
        kernel,
        in_specs=[vmem] * (1 + len(operands)) + spaces,
        out_specs=vmem,
        out_shape=jax.ShapeDtypeStruct(m.shape, bf16),
        compiler_params=pltpu.CompilerParams(vmem_limit_bytes=8 * MEG),
        name="hop",
    )(m, *operands, *after)


def stage_kernel(from_ref, *refs):
    refs[-1][...] = from_ref[...]


def stage_call(terms, after):
    vmem = pl.BlockSpec(memory_space=pltpu.VMEM)
    after, spaces = waits(after)
    return pl.pallas_call(
        stage_kernel,
        in_specs=[vmem] + spaces,
        out_specs=vmem,
        out_shape=jax.ShapeDtypeStruct(terms.shape, terms.dtype),
        compiler_params=pltpu.CompilerParams(vmem_limit_bytes=16 * MEG),
        name="stage",
    )(terms, *after)


def finish_kernel(span, size, shape, here_ref, term_ref, other_ref, *refs):
    entries, at = [], 0
    for count in shape:
        entries.append(refs[at:at + count])
        at += count
    outs = refs[at:at + size]
    depth, tokens, width = term_ref.shape
    chunk = tokens // size
    heads = range(span[0], sum(span))
    here = here_ref[0]
    position = here_ref[1]
    zero = jnp.zeros((WIDE, WIDE), bf16)
    odd = (position & 1) == 1
    pair = position >> 1
    carries = []
    for h in heads:
        came = []
        for m, options in enumerate(entries):
            entry = zero
            for j, ref in enumerate(options):
                mine = ((pair >> m) & 1 == 1) & ((pair & ((1 << m) - 1)) == j)
                entry = jnp.where(mine, ref[h], entry)
            came.append(entry)
        wide = jnp.concatenate(came, axis=1)
        ahead = mxu(other_ref[h, :, WIDE:], wide).astype(bf16)
        carries.append(jnp.concatenate(
            [jnp.where(odd, other_ref[h, :, :WIDE], zero)]
            + [
                jnp.where(odd, ahead[:, m * WIDE:(m + 1) * WIDE], x) for m, x in enumerate(came)
            ],
            axis=0,
        ))
    for d in range(size):
        toks = aligned(here ^ d, chunk)

        def head(h):
            part = slice(h * WIDE, (h + 1) * WIDE)
            far = jnp.concatenate([term_ref[i, toks, part] for i in range(1, depth)], axis=1)
            total = mxu(far, carries[h - span[0]])
            yield
            out = slice((h - span[0]) * WIDE, (h - span[0] + 1) * WIDE)
            outs[d][:, out] = (total + term_ref[0, toks, part].astype(f32)).astype(bf16)

        together([head(h) for h in heads])


def finish_call(span, size, here, terms, other, entries, after):
    depth, tokens, width = terms.shape
    smem = pl.BlockSpec(memory_space=pltpu.SMEM)
    vmem = pl.BlockSpec(memory_space=pltpu.VMEM)
    shape = [len(e) for e in entries]
    flat = [x for e in entries for x in e]
    after, spaces = waits(after)

    def kernel(*refs):
        used = 3 + len(flat)
        finish_kernel(span, size, shape, *refs[:used], *refs[used + len(after):])

    return pl.pallas_call(
        kernel,
        in_specs=[smem] + [vmem] * (2 + len(flat)) + spaces,
        out_specs=[vmem] * size,
        out_shape=[jax.ShapeDtypeStruct((tokens // size, span[1] * WIDE), bf16)] * size,
        compiler_params=pltpu.CompilerParams(vmem_limit_bytes=FINISH * MEG),
        name="finish",
    )(here, terms, other, *flat, *after)


def gather_kernel(first, heads, sources, place_ref, *refs):
    parts, (out_ref, mark_ref, sems) = refs[:len(sources)], refs[-3:]
    mark_ref[...] = jnp.zeros_like(mark_ref)
    here = place_ref[0]
    copies = []
    for i, (d, ref) in enumerate(zip(sources, parts)):
        col = pl.multiple_of(((here ^ d) * heads + first) * WIDE, WIDE)
        where = out_ref.at[:, pl.ds(col, ref.shape[1])]
        copies.append(pltpu.make_async_copy(ref, where, sems.at[i]))
        copies[-1].start()
    for c in copies:
        c.wait()


def gather_call(first, heads, size, place, parts, before, after):
    sources, parts = zip(*parts)
    count = len(parts)
    vmem = pl.BlockSpec(memory_space=pltpu.VMEM)
    hbm = pl.BlockSpec(memory_space=pltpu.HBM)
    after, spaces = waits(after)
    kept = [] if before is None else [before]

    def kernel(*refs):
        gather_kernel(first, heads, sources, *refs)

    return pl.pallas_call(
        kernel,
        in_specs=[pl.BlockSpec(memory_space=pltpu.SMEM)] + [vmem] * count + [hbm] * len(kept)
        + spaces,
        out_specs=[hbm, vmem],
        out_shape=[
            jax.ShapeDtypeStruct((parts[0].shape[0], heads * size * WIDE), bf16),
            jax.ShapeDtypeStruct((8, WIDE), f32),
        ],
        input_output_aliases={1 + count: 0} if kept else {},
        scratch_shapes=[pltpu.SemaphoreType.DMA((count,))],
        compiler_params=pltpu.CompilerParams(vmem_limit_bytes=GATHER * MEG),
        name="gather",
    )(place, *parts, *kept, *after)


ORDER = ("l0", "l1", "p0", "t0", "h01", "p1", "h02", "h11", "f00")
ORDER += ("h12", "a00", "f10", "b00", "a10", "b10")


def order(groups, steps):
    names = dict(l="local", p="pair", t="stage", h="hop", f="finish", g="gather", a="some", b="rest")
    if steps == 3:
        return [(names[x[0]], int(x[1]), int(x[2:] or 0)) for x in ORDER]
    out = [("local", g, 0) for g in range(groups)] + [("pair", g, 0) for g in range(groups)]
    out += [("hop", g, step) for step in range(1, steps) for g in range(groups)]
    out += [("finish", g, i) for g in range(groups) for i in range(PARTS)]
    return out + [("gather", g, i) for g in range(groups) for i in range(PARTS)]


def per_device(queries, key_rows, value_rows, log_decay, write_rate, level_weights, block_levels):
    size = lax.axis_size("ctx")
    bits = size.bit_length() - 1
    width = lax.axis_size("head")
    position = lax.axis_index("ctx").astype(jnp.int32)
    place = lax.axis_index("head").astype(jnp.int32)
    here = jnp.stack([place, position])
    flag = (position & 1).reshape(1)
    heads = log_decay.shape[1]
    groups = split(heads, SHARES)
    pairs = size // 2
    steps = [(m, j) for m in range(pairs.bit_length() - 1) for j in range(1 << m)]

    def swap(low, array):
        to = list(range(pairs))
        for p in low:
            to[p], to[p + 1] = p + 1, p
        return lax.ppermute(array, "ctx", [(i, 2 * to[i >> 1] + (i & 1)) for i in range(size)])

    runs, others, terms, states, solved = {}, {}, {}, {}, []
    entries = [[] for _ in groups]
    pieces = {}
    after = []

    def local(g):
        runs[g], terms[g], mark, *kept = local_call(
            groups[g], heads, bits, block_levels, level_weights.T, solved[0] if solved else None,
            [log_decay.T, write_rate.T, key_rows], queries, value_rows, after,
        )
        if kept:
            solved.append(kept)
        others[g] = lax.ppermute(runs[g], "ctx", [(i, i ^ 1) for i in range(size)])
        return mark, pltpu.VMEM

    def pair(g):
        states[g] = pair_call(flag, runs[g], others[g], after)
        return states[g][1], pltpu.VMEM

    def hop(g, step):
        m, j = steps[step]
        s, t = states[g]
        if j:
            sent = hop_call(t, None, [entries[g][m][j - 1]], after)
        elif m:
            sent = hop_call(t, s, [e[-1] for e in entries[g]], after)
        else:
            sent = s
        if j == 0:
            entries[g].append([])
        low = [p for p in range(pairs) if p % (2 << m) == (1 << m) + j - 1]
        entries[g][m].append(swap(low, sent))
        return sent, pltpu.VMEM

    def stage(g):
        terms[g] = stage_call(terms[g], after)
        return terms[g], pltpu.VMEM

    def span_of(g, part):
        return split(groups[g][1], (1,) * PARTS)[part]

    def finish(g, part):
        outs = finish_call(
            span_of(g, part), width, here, terms[g], others[g], entries[g], after
        )
        for d in range(width):
            pairing = [(i, i ^ d) for i in range(width)]
            pieces[g, part, d] = outs[d] if d == 0 else lax.ppermute(outs[d], "head", pairing)
        return outs[0], pltpu.VMEM

    def gather(g, part, out, ds):
        parts = [(d, pieces[g, part, d]) for d in ds]
        first = groups[g][0] + span_of(g, part)[0]
        return gather_call(first, heads, width, place.reshape(1), parts, out, after)

    out = None
    for name, g, step in order(len(groups), len(steps)):
        if name == "local":
            token = local(g)
        elif name == "pair":
            token = pair(g)
            hop(g, 0)
        elif name == "stage":
            token = stage(g)
        elif name == "hop":
            token = hop(g, step)
        elif name == "finish":
            token = finish(g, step)
        else:
            cut = width - 1
            ds = dict(some=range(cut), rest=range(cut, width)).get(name, range(width))
            out, mark = gather(g, step, out, ds)
            token = mark, pltpu.VMEM
        after = [token]
    return out


def solution(mesh):
    wide = P("ctx", "head")
    return jax.shard_map(
        per_device,
        mesh=mesh,
        in_specs=(wide, wide, wide, wide, wide, wide, P("ctx")),
        out_specs=P(("ctx", "head"), None),
        check_vma=False,
    )
```

```python
import jax
import jax.numpy as jnp
from jax import lax
from jax.sharding import PartitionSpec as P
from jax.experimental import pallas as pl
from jax.experimental.pallas import tpu as pltpu

BLOCK = 64
WIDE = 128
LEVELS = 5
SHARES = (8, 8)
f32 = jnp.float32
bf16 = jnp.bfloat16
MEG = 1024 * 1024
FINISH = 16
LOCAL = 62.25
PARTS = 1
SIDE = 4
GATHER = 8


def mxu(a, b):
    return lax.dot_general(a, b, (((1,), (0,)), ((), ())), preferred_element_type=f32)


def mxu_t(a, b):
    return lax.dot_general(a, b, (((1,), (1,)), ((), ())), preferred_element_type=f32)


def halves(x):
    hi = x.astype(bf16)
    return hi, (x - hi.astype(f32)).astype(bf16)


def together(live):
    while live:
        live = [g for g in live if next(g, g) is not g]


def repeat(count, body, unroll):
    while count % unroll:
        unroll -= 1

    def step(i, _):
        together([body(i * unroll + j) for j in range(unroll)])
        return 0

    lax.fori_loop(0, count // unroll, step, 0)


def split(heads, shares):
    counts = [heads * share // sum(shares) for share in shares]
    counts[-1] = heads - sum(counts[:-1])
    return [(sum(counts[:g]), n) for g, n in enumerate(counts)]


def aligned(index, size):
    return pl.ds(pl.multiple_of(index * size, size), size)


def left_half():
    return lax.broadcasted_iota(jnp.int32, (BLOCK, WIDE), 1) < BLOCK


def diagonal(x, left):
    zero = jnp.zeros_like(x)
    return jnp.concatenate([jnp.where(left, x, zero), jnp.where(left, zero, x)], axis=0)


def column(table, lane, at):
    picked = jnp.sum(jnp.where(lane == at, table, 0.0), axis=1, keepdims=True)
    return jnp.broadcast_to(picked, (BLOCK, WIDE))


def local_kernel(solve, span, heads, depth, levels_ref, *refs):
    first, count = span
    names = ["weight", "row", "col", "kn", "t", "q", "v"]
    if solve:
        names = ["weight", "ld", "wr", "k", "q", "v"]
    inputs, refs = dict(zip(names, refs)), refs[len(names):]
    run_ref, term_hbm, mark_ref, refs = *refs[:3], refs[3:]
    mark_ref[...] = jnp.zeros_like(mark_ref)
    if solve:
        row_s, colg_s, kn_hbm, t_hbm, refs = *refs[:4], refs[4:]
        ld_s, wr_s, k_s, low_s, inv_s, colb_s, key_sem, refs = *refs[:7], refs[7:]
    else:
        row_s, colg_s = inputs["row"], inputs["col"]
    (
        weight_s, q_s, v_s, kn_s, gram_s, scale_s, m_s, fall_s, s_s, qt_s, near_s, p_s, term_s, copy_sem,
        pair_sem, keep_sem, step_sem,
    ) = refs
    tokens = q_s.shape[0]
    pairs = tokens // WIDE
    units = heads * pairs
    blocks = tokens // BLOCK
    lanes = 2 * units
    across = heads if solve else count
    mine = slice(first * WIDE, (first + count) * WIDE)

    loads = {"weight": (inputs["weight"], weight_s)}
    if solve:
        loads.update(ld=(inputs["ld"], ld_s), wr=(inputs["wr"], wr_s))

    def pair_copies(p):
        toks = aligned(p, WIDE)
        copies = [
            (inputs["q"].at[toks, mine], q_s.at[toks, :]),
            (inputs["v"].at[toks, mine], v_s.at[toks, :]),
        ]
        if not solve:
            size = count * BLOCK
            at = pl.ds(pl.multiple_of((p * heads + first) * BLOCK, BLOCK), size)
            copies += [
                (inputs["kn"].at[first:first + count, toks, :], kn_s.at[:, toks, :]),
                (inputs["t"].at[at, :], gram_s.at[aligned(p, size), :]),
            ]
        return [
            pltpu.make_async_copy(x, y, pair_sem.at[p, i]) for i, (x, y) in enumerate(copies)
        ]

    if solve:
        for i, name in enumerate(("q", "v")):
            loads[name] = (inputs[name].at[:, mine], (q_s, v_s)[i])

    loads = {
        name: pltpu.make_async_copy(x, y, copy_sem.at[i])
        for i, (name, (x, y)) in enumerate(loads.items())
    }
    if solve:
        quarter = k_s.shape[1] // 4

        def key_copy(i):
            part = aligned(i, quarter)
            return pltpu.make_async_copy(inputs["k"].at[:, part], k_s.at[:, part], key_sem.at[i])

        loads["ld"].start()
        loads["wr"].start()
        for i in range(4):
            key_copy(i).start()
    if not solve:
        for p in range(pairs):
            for c in pair_copies(p):
                c.start()
    for name, c in loads.items():
        if name not in ("ld", "wr"):
            c.start()

    left = left_half()
    ri = lax.broadcasted_iota(jnp.int32, (WIDE, WIDE), 0)
    ci = lax.broadcasted_iota(jnp.int32, (WIDE, WIDE), 1)

    def inverses():
        tri = jnp.where((ri <= ci) & ((ri >= BLOCK) == (ci >= BLOCK)), 1.0, 0.0)
        def by_unit(x):
            return jnp.concatenate([x[:, p * WIDE:(p + 1) * WIDE] for p in range(pairs)], axis=0)

        loads["ld"].wait()
        loads["wr"].wait()
        grow = lax.dot_general(
            by_unit(ld_s[...]), tri, (((1,), (0,)), ((), ())),
            precision=lax.Precision.HIGHEST, preferred_element_type=f32,
        )
        row_s[...] = grow
        gcol = grow.T
        bcol = by_unit(wr_s[...]).T
        colg_s[...] = jnp.concatenate([gcol[:BLOCK], gcol[BLOCK:]], axis=1)
        colb_s[...] = jnp.concatenate([bcol[:BLOCK], bcol[BLOCK:]], axis=1)

        def keys(h):
            cols = aligned(h, WIDE)
            kf = k_s[:, cols].astype(f32)
            total = jnp.sum(kf * kf, axis=1, keepdims=True)
            yield
            kn = (kf * lax.rsqrt(total + 1e-6)).astype(bf16)
            kn_s[h] = kn
            grams = []
            for p in range(pairs):
                kp = kn[p * WIDE:(p + 1) * WIDE]
                grams.append(mxu_t(kp, kp))
            yield
            for p, g in enumerate(grams):
                gram_s[aligned(p * heads + h, BLOCK), :] = jnp.where(left, g[:BLOCK], g[BLOCK:])

        def key_group(i, _):
            key_copy(i).wait()
            together([keys(i * (heads // 4) + j) for j in range(heads // 4)])
            return 0

        lax.fori_loop(0, 4, key_group, 0)

        def to_lanes(i):
            a = gram_s[pl.ds(i, units, stride=BLOCK), :].T
            yield
            g = jnp.concatenate([a[:BLOCK], a[BLOCK:]], axis=1)
            gi = colg_s[pl.ds(i, 1), :]
            bi = colb_s[pl.ds(i, 1), :]
            e = jnp.exp(gi - colg_s[...])
            yield
            low_s[i] = g * (bi * e)
            inv_s[i] = jnp.zeros_like(g)

        repeat(BLOCK, to_lanes, 16)

        sub = lax.broadcasted_iota(jnp.int32, (8, lanes), 0)

        def solve(bi, _):
            i0 = bi * 8

            def columns(cb, _):
                c = aligned(cb, 8)

                def step(jb, acc):
                    acc = list(acc)
                    for jj in range(8):
                        j = jb * 8 + jj
                        t = inv_s[j, c, :]
                        for r in range(8):
                            acc[r] = acc[r] - low_s[i0 + r, pl.ds(j, 1), :] * t
                    return tuple(acc)

                on = cb == bi
                acc = tuple(jnp.where((sub == r) & on, 1.0, 0.0) for r in range(8))
                acc = list(lax.fori_loop(cb, bi, step, acc))
                for r in range(8):
                    inv_s[i0 + r, c, :] = acc[r]
                    for s in range(r + 1, 8):
                        acc[s] = acc[s] - low_s[i0 + s, pl.ds(i0 + r, 1), :] * acc[r]
                return 0

            lax.fori_loop(0, bi + 1, columns, 0)
            return 0

        lax.fori_loop(0, BLOCK // 8, solve, 0)

        def from_lanes(i):
            t = inv_s[i] * colb_s[...]
            a = jnp.concatenate([t[:, :units], t[:, units:]], axis=0).T
            yield
            gram_s[pl.ds(i, units, stride=BLOCK), :] = a

        repeat(BLOCK, from_lanes, 16)

    kept = []
    if solve:
        inverses()
        kept = [(kn_s, kn_hbm), (gram_s, t_hbm)]
        kept = [pltpu.make_async_copy(x, y, keep_sem.at[i]) for i, (x, y) in enumerate(kept)]
        for c in kept:
            c.start()
    clane = lax.broadcasted_iota(jnp.int32, (BLOCK, lanes), 1)
    lane = lax.broadcasted_iota(jnp.int32, (BLOCK, WIDE), 1)
    row64 = lax.broadcasted_iota(jnp.int32, (BLOCK, WIDE), 0)
    keep = row64 >= jnp.where(left, lane, lane - BLOCK)
    eye = ri == ci

    def unit(p, h):
        i = p * count + h
        u = p * heads + first + h
        grow = row_s[pl.ds(u, 1), :]
        gs = [column(colg_s[...], clane, u), column(colg_s[...], clane, u + units)]
        kn = kn_s[h, aligned(p, WIDE), :]
        v = v_s[aligned(p, WIDE), aligned(h, WIDE)]
        q = q_s[aligned(p, WIDE), aligned(h, WIDE)]
        qk = mxu_t(q, kn)
        t1 = gram_s[aligned(p * across + h, BLOCK), :]
        t2 = t1 * jnp.exp(grow)
        a_hi, a_lo = halves(diagonal(t1, left))
        b_hi, b_lo = halves(diagonal(t2, left))
        wv = mxu(jnp.concatenate([a_hi, a_lo], axis=1), jnp.concatenate([v, v], axis=0))
        wk = mxu(jnp.concatenate([b_hi, b_lo], axis=1), jnp.concatenate([kn, kn], axis=0))
        knt = kn.astype(f32).T.astype(bf16)
        decay = jnp.exp(jnp.where(keep, jnp.where(left, gs[0], gs[1]) - grow, -1e30))
        yield
        score = diagonal(jnp.where(left, qk[:BLOCK], qk[BLOCK:]) * decay, left).astype(bf16)
        w = jnp.concatenate([wv, wk], axis=1)
        kk = jnp.concatenate([knt, knt], axis=1)
        outs = []
        for half, g in enumerate(gs):
            end = g[BLOCK - 1:, :]
            tail = jnp.exp(end - g)
            part = w[half * BLOCK:(half + 1) * BLOCK] * jnp.concatenate([tail, tail], axis=1)
            hi, lo = halves(part)
            none = jnp.zeros_like(hi)
            stack = [hi, none, lo, none] if half == 0 else [none, hi, none, lo]
            outs.append((end, mxu(kk, jnp.concatenate(stack, axis=0))))
        ys = mxu(score, w.astype(bf16))
        yield
        for half, (end, y) in enumerate(outs):
            s_s[2 * p + half, h] = y[:, :WIDE]
            m_s[2 * p + half, h] = y[:, WIDE:].astype(bf16)
            fall_s[2 * p + half, pl.ds(h, 1), :] = jnp.exp(end)
        near_s[i] = ys[:, :WIDE]
        eg = jnp.exp(jnp.concatenate(gs, axis=0))
        qt_s[i] = (eg * q.astype(f32) - ys[:, WIDE:]).astype(bf16)

    if solve:
        loads["q"].wait()
        loads["v"].wait()

    def pair_units(p, _):
        if not solve:
            for c in pair_copies(p):
                c.wait()
        repeat(count, lambda h: unit(p, h), 8)
        return 0

    lax.fori_loop(0, pairs, pair_units, 0)

    loads["weight"].wait()
    slots = weight_s.shape[0]
    level = lax.rem(lax.broadcasted_iota(jnp.int32, (BLOCK, slots), 1), LEVELS)
    weight = weight_s[...].T
    for b in range(blocks):
        toks = slice(b * BLOCK, (b + 1) * BLOCK)
        scale_s[toks, :] = jnp.where(level < levels_ref[b], weight[toks], 0.0)

    def term_copy(b):
        toks = aligned(b, BLOCK)
        return pltpu.make_async_copy(term_s.at[b], term_hbm.at[:, toks, :], step_sem.at[b])

    def write(b, h, near, rows):
        cols = pl.ds(h * WIDE, WIDE)
        scale = scale_s[aligned(b, BLOCK), :]
        for i in range(1 + depth):
            at = (first + h) * LEVELS + i
            term_s[b, i, :, cols] = ((rows if i else near) * scale[:, at:at + 1]).astype(bf16)

    for h in range(count):
        p_s[h, :, :WIDE] = s_s[0, h]
        p_s[h, :, WIDE:] = jnp.where(eye, fall_s[0, h:h + 1, :], 0.0) - m_s[0, h].astype(f32)
        write(0, h, near_s[h, :BLOCK, :], qt_s[h, :BLOCK, :].astype(f32))
    term_copy(0).start()

    def scan(b, _):
        half = aligned(b % 2, BLOCK)

        def advance(h):
            i = (b // 2) * count + h
            both = mxu(
                jnp.concatenate([m_s[b, h], qt_s[i, half, :]], axis=0), p_s[h].astype(bf16)
            )
            yield
            fall = fall_s[b, h:h + 1, :]
            n, o = both[:WIDE], both[WIDE:]
            p_s[h, :, :WIDE] = fall * p_s[h, :, :WIDE] + s_s[b, h] - n[:, :WIDE]
            p_s[h, :, WIDE:] = fall * p_s[h, :, WIDE:] - n[:, WIDE:]
            write(b, h, near_s[i, half, :] + o[:, :WIDE], o[:, WIDE:])

        for h in range(0, count, SIDE):
            together([advance(h + j) for j in range(min(SIDE, count - h))])
        term_copy(b).start()
        return 0

    lax.fori_loop(1, blocks, scan, 0)
    for h in range(count):
        run_ref[h] = p_s[h].astype(bf16)
    for c in kept:
        c.wait()
    for b in range(blocks):
        term_copy(b).wait()


def local_call(span, heads, depth, levels, weights, solved, inputs, q, v, after):
    tokens = q.shape[0]
    first, count = span
    pairs = tokens // WIDE
    units = heads * pairs
    blocks = tokens // BLOCK
    solve = solved is None
    smem = pl.BlockSpec(memory_space=pltpu.SMEM)
    vmem = pl.BlockSpec(memory_space=pltpu.VMEM)
    hbm = pl.BlockSpec(memory_space=pltpu.HBM)
    after, spaces = waits(after)
    out_specs = [vmem, hbm, vmem]
    out_shape = [
        jax.ShapeDtypeStruct((count, WIDE, 2 * WIDE), bf16),
        jax.ShapeDtypeStruct((1 + depth, tokens, count * WIDE), bf16),
        jax.ShapeDtypeStruct((8, WIDE), f32),
    ]
    scratch = []
    if solve:
        operands = [weights, *inputs, q, v]
        in_specs = [hbm] * 6
        out_specs += [vmem, vmem, hbm, hbm]
        out_shape += [
            jax.ShapeDtypeStruct((units, WIDE), f32),
            jax.ShapeDtypeStruct((BLOCK, 2 * units), f32),
            jax.ShapeDtypeStruct((heads, tokens, WIDE), bf16),
            jax.ShapeDtypeStruct((units * BLOCK, WIDE), f32),
        ]
        scratch = [
            pltpu.VMEM(inputs[0].shape, f32),
            pltpu.VMEM(inputs[1].shape, f32),
            pltpu.VMEM(inputs[2].shape, bf16),
            pltpu.VMEM((BLOCK, BLOCK, 2 * units), f32),
            pltpu.VMEM((BLOCK, BLOCK, 2 * units), f32),
            pltpu.VMEM((BLOCK, 2 * units), f32),
            pltpu.SemaphoreType.DMA((4,)),
        ]
    else:
        operands = [weights, *solved, q, v]
        in_specs = [hbm, vmem, vmem, hbm, hbm, hbm, hbm]
    across = heads if solve else count

    def kernel(*refs):
        used = 1 + len(operands)
        local_kernel(solve, span, heads, depth, *refs[:used], *refs[used + len(after):])

    return pl.pallas_call(
        kernel,
        in_specs=[smem] + in_specs + spaces,
        out_specs=out_specs,
        out_shape=out_shape,
        scratch_shapes=scratch
        + [
            pltpu.VMEM(weights.shape, f32),
            pltpu.VMEM((tokens, count * WIDE), bf16),
            pltpu.VMEM((tokens, count * WIDE), bf16),
            pltpu.VMEM((across, tokens, WIDE), bf16),
            pltpu.VMEM((across * pairs * BLOCK, WIDE), f32),
            pltpu.VMEM((tokens, weights.shape[0]), f32),
            pltpu.VMEM((blocks, count, WIDE, WIDE), bf16),
            pltpu.VMEM((blocks, count, WIDE), f32),
            pltpu.VMEM((blocks, count, WIDE, WIDE), f32),
            pltpu.VMEM((pairs * count, WIDE, WIDE), bf16),
            pltpu.VMEM((pairs * count, WIDE, WIDE), f32),
            pltpu.VMEM((count, WIDE, 2 * WIDE), f32),
            pltpu.VMEM((blocks, 1 + depth, BLOCK, count * WIDE), bf16),
            pltpu.SemaphoreType.DMA((5,)),
            pltpu.SemaphoreType.DMA((pairs, 4)),
            pltpu.SemaphoreType.DMA((2,)),
            pltpu.SemaphoreType.DMA((blocks,)),
        ],
        compiler_params=pltpu.CompilerParams(vmem_limit_bytes=int(LOCAL * MEG)),
        name="local",
    )(levels, *operands, *after)


def waits(after):
    return [x for x, _ in after], [pl.BlockSpec(memory_space=space) for _, space in after]


def pair_kernel(flag_ref, own_ref, other_ref, *rest):
    s_ref, m_ref = rest[-2:]
    heads = own_ref.shape[0]
    upper = flag_ref[0] == 1

    def head(h):
        own = own_ref[h]
        other = other_ref[h]
        late = jnp.where(upper, own, other)
        early = jnp.where(upper, other, own)
        both = mxu(late[:, WIDE:], early)
        yield
        s_ref[h] = (both[:, :WIDE] + late[:, :WIDE].astype(f32)).astype(bf16)
        m_ref[h] = both[:, WIDE:].astype(bf16)

    together([head(h) for h in range(heads)])


def pair_call(flag, own, other, after):
    square = jax.ShapeDtypeStruct((own.shape[0], WIDE, WIDE), bf16)
    vmem = pl.BlockSpec(memory_space=pltpu.VMEM)
    after, spaces = waits(after)
    return pl.pallas_call(
        pair_kernel,
        in_specs=[pl.BlockSpec(memory_space=pltpu.SMEM), vmem, vmem]
        + spaces,
        out_specs=[vmem, vmem],
        out_shape=[square, square],
        compiler_params=pltpu.CompilerParams(vmem_limit_bytes=8 * MEG),
        name="pair",
    )(flag, own, other, *after)


def hop_kernel(m_ref, *refs):
    *entry_refs, out_ref = refs

    def head(h):
        entry = entry_refs[1][h]
        for ref in entry_refs[2:]:
            entry = (entry.astype(f32) + ref[h].astype(f32)).astype(bf16)
        o = mxu(m_ref[h], entry)
        yield
        if entry_refs[0] is not None:
            o = o + entry_refs[0][h].astype(f32)
        out_ref[h] = o.astype(bf16)

    together([head(h) for h in range(m_ref.shape[0])])


def hop_call(m, s, entries, after):
    vmem = pl.BlockSpec(memory_space=pltpu.VMEM)
    operands = ([] if s is None else [s]) + entries

    after, spaces = waits(after)

    def kernel(m_ref, *refs):
        used = refs[:len(operands)] + refs[-1:]
        hop_kernel(m_ref, *(used if s is not None else (None,) + used))

    return pl.pallas_call(
        kernel,
        in_specs=[vmem] * (1 + len(operands)) + spaces,
        out_specs=vmem,
        out_shape=jax.ShapeDtypeStruct(m.shape, bf16),
        compiler_params=pltpu.CompilerParams(vmem_limit_bytes=8 * MEG),
        name="hop",
    )(m, *operands, *after)


def stage_kernel(from_ref, *refs):
    refs[-1][...] = from_ref[...]


def stage_call(terms, after):
    vmem = pl.BlockSpec(memory_space=pltpu.VMEM)
    after, spaces = waits(after)
    return pl.pallas_call(
        stage_kernel,
        in_specs=[vmem] + spaces,
        out_specs=vmem,
        out_shape=jax.ShapeDtypeStruct(terms.shape, terms.dtype),
        compiler_params=pltpu.CompilerParams(vmem_limit_bytes=16 * MEG),
        name="stage",
    )(terms, *after)


def finish_kernel(span, size, shape, here_ref, term_ref, other_ref, *refs):
    entries, at = [], 0
    for count in shape:
        entries.append(refs[at:at + count])
        at += count
    outs = refs[at:at + size]
    depth, tokens, width = term_ref.shape
    chunk = tokens // size
    heads = range(span[0], sum(span))
    here = here_ref[0]
    position = here_ref[1]
    zero = jnp.zeros((WIDE, WIDE), bf16)
    odd = (position & 1) == 1
    pair = position >> 1
    carries = []
    for h in heads:
        came = []
        for m, options in enumerate(entries):
            entry = zero
            for j, ref in enumerate(options):
                mine = ((pair >> m) & 1 == 1) & ((pair & ((1 << m) - 1)) == j)
                entry = jnp.where(mine, ref[h], entry)
            came.append(entry)
        wide = jnp.concatenate(came, axis=1)
        ahead = mxu(other_ref[h, :, WIDE:], wide).astype(bf16)
        carries.append(jnp.concatenate(
            [jnp.where(odd, other_ref[h, :, :WIDE], zero)]
            + [
                jnp.where(odd, ahead[:, m * WIDE:(m + 1) * WIDE], x) for m, x in enumerate(came)
            ],
            axis=0,
        ))
    for d in range(size):
        toks = aligned(here ^ d, chunk)

        def head(h):
            part = slice(h * WIDE, (h + 1) * WIDE)
            far = jnp.concatenate([term_ref[i, toks, part] for i in range(1, depth)], axis=1)
            total = mxu(far, carries[h - span[0]])
            yield
            out = slice((h - span[0]) * WIDE, (h - span[0] + 1) * WIDE)
            outs[d][:, out] = (total + term_ref[0, toks, part].astype(f32)).astype(bf16)

        together([head(h) for h in heads])


def finish_call(span, size, here, terms, other, entries, after):
    depth, tokens, width = terms.shape
    smem = pl.BlockSpec(memory_space=pltpu.SMEM)
    vmem = pl.BlockSpec(memory_space=pltpu.VMEM)
    shape = [len(e) for e in entries]
    flat = [x for e in entries for x in e]
    after, spaces = waits(after)

    def kernel(*refs):
        used = 3 + len(flat)
        finish_kernel(span, size, shape, *refs[:used], *refs[used + len(after):])

    return pl.pallas_call(
        kernel,
        in_specs=[smem] + [vmem] * (2 + len(flat)) + spaces,
        out_specs=[vmem] * size,
        out_shape=[jax.ShapeDtypeStruct((tokens // size, span[1] * WIDE), bf16)] * size,
        compiler_params=pltpu.CompilerParams(vmem_limit_bytes=FINISH * MEG),
        name="finish",
    )(here, terms, other, *flat, *after)


def gather_kernel(first, heads, sources, place_ref, *refs):
    parts, (out_ref, mark_ref, sems) = refs[:len(sources)], refs[-3:]
    mark_ref[...] = jnp.zeros_like(mark_ref)
    here = place_ref[0]
    copies = []
    for i, (d, ref) in enumerate(zip(sources, parts)):
        col = pl.multiple_of(((here ^ d) * heads + first) * WIDE, WIDE)
        where = out_ref.at[:, pl.ds(col, ref.shape[1])]
        copies.append(pltpu.make_async_copy(ref, where, sems.at[i]))
        copies[-1].start()
    for c in copies:
        c.wait()


def gather_call(first, heads, size, place, parts, before, after):
    sources, parts = zip(*parts)
    count = len(parts)
    vmem = pl.BlockSpec(memory_space=pltpu.VMEM)
    hbm = pl.BlockSpec(memory_space=pltpu.HBM)
    after, spaces = waits(after)
    kept = [] if before is None else [before]

    def kernel(*refs):
        gather_kernel(first, heads, sources, *refs)

    return pl.pallas_call(
        kernel,
        in_specs=[pl.BlockSpec(memory_space=pltpu.SMEM)] + [vmem] * count + [hbm] * len(kept)
        + spaces,
        out_specs=[hbm, vmem],
        out_shape=[
            jax.ShapeDtypeStruct((parts[0].shape[0], heads * size * WIDE), bf16),
            jax.ShapeDtypeStruct((8, WIDE), f32),
        ],
        input_output_aliases={1 + count: 0} if kept else {},
        scratch_shapes=[pltpu.SemaphoreType.DMA((count,))],
        compiler_params=pltpu.CompilerParams(vmem_limit_bytes=GATHER * MEG),
        name="gather",
    )(place, *parts, *kept, *after)


ORDER = ("l0", "l1", "p0", "h01", "p1", "h02", "h11", "t0", "f00")
ORDER += ("h12", "t1", "a00", "f10", "b00", "a10", "b10")


def order(groups, steps):
    names = dict(l="local", p="pair", t="stage", h="hop", f="finish", g="gather", a="some", b="rest")
    if steps == 3:
        return [(names[x[0]], int(x[1]), int(x[2:] or 0)) for x in ORDER]
    out = [("local", g, 0) for g in range(groups)] + [("pair", g, 0) for g in range(groups)]
    out += [("hop", g, step) for step in range(1, steps) for g in range(groups)]
    out += [("finish", g, i) for g in range(groups) for i in range(PARTS)]
    return out + [("gather", g, i) for g in range(groups) for i in range(PARTS)]


def per_device(queries, key_rows, value_rows, log_decay, write_rate, level_weights, block_levels):
    size = lax.axis_size("ctx")
    bits = size.bit_length() - 1
    width = lax.axis_size("head")
    position = lax.axis_index("ctx").astype(jnp.int32)
    place = lax.axis_index("head").astype(jnp.int32)
    here = jnp.stack([place, position])
    flag = (position & 1).reshape(1)
    heads = log_decay.shape[1]
    groups = split(heads, SHARES)
    pairs = size // 2
    steps = [(m, j) for m in range(pairs.bit_length() - 1) for j in range(1 << m)]

    def swap(low, array):
        to = list(range(pairs))
        for p in low:
            to[p], to[p + 1] = p + 1, p
        return lax.ppermute(array, "ctx", [(i, 2 * to[i >> 1] + (i & 1)) for i in range(size)])

    runs, others, terms, states, solved = {}, {}, {}, {}, []
    entries = [[] for _ in groups]
    pieces = {}
    after = []

    def local(g):
        runs[g], terms[g], mark, *kept = local_call(
            groups[g], heads, bits, block_levels, level_weights.T, solved[0] if solved else None,
            [log_decay.T, write_rate.T, key_rows], queries, value_rows, after,
        )
        if kept:
            solved.append(kept)
        others[g] = lax.ppermute(runs[g], "ctx", [(i, i ^ 1) for i in range(size)])
        return mark, pltpu.VMEM

    def pair(g):
        states[g] = pair_call(flag, runs[g], others[g], after)
        return states[g][1], pltpu.VMEM

    def hop(g, step):
        m, j = steps[step]
        s, t = states[g]
        if j:
            sent = hop_call(t, None, [entries[g][m][j - 1]], after)
        elif m:
            sent = hop_call(t, s, [e[-1] for e in entries[g]], after)
        else:
            sent = s
        if j == 0:
            entries[g].append([])
        low = [p for p in range(pairs) if p % (2 << m) == (1 << m) + j - 1]
        entries[g][m].append(swap(low, sent))
        return sent, pltpu.VMEM

    def stage(g):
        terms[g] = stage_call(terms[g], after)
        return terms[g], pltpu.VMEM

    def span_of(g, part):
        return split(groups[g][1], (1,) * PARTS)[part]

    def finish(g, part):
        outs = finish_call(
            span_of(g, part), width, here, terms[g], others[g], entries[g], after
        )
        for d in range(width):
            pairing = [(i, i ^ d) for i in range(width)]
            pieces[g, part, d] = outs[d] if d == 0 else lax.ppermute(outs[d], "head", pairing)
        return outs[0], pltpu.VMEM

    def gather(g, part, out, ds):
        parts = [(d, pieces[g, part, d]) for d in ds]
        first = groups[g][0] + span_of(g, part)[0]
        return gather_call(first, heads, width, place.reshape(1), parts, out, after)

    out = None
    for name, g, step in order(len(groups), len(steps)):
        if name == "local":
            token = local(g)
        elif name == "pair":
            token = pair(g)
            hop(g, 0)
        elif name == "stage":
            token = stage(g)
        elif name == "hop":
            token = hop(g, step)
        elif name == "finish":
            token = finish(g, step)
        else:
            cut = width - 1
            ds = dict(some=range(cut), rest=range(cut, width)).get(name, range(width))
            out, mark = gather(g, step, out, ds)
            token = mark, pltpu.VMEM
        after = [token]
    return out


def solution(mesh):
    wide = P("ctx", "head")
    return jax.shard_map(
        per_device,
        mesh=mesh,
        in_specs=(wide, wide, wide, wide, wide, wide, P("ctx")),
        out_specs=P(("ctx", "head"), None),
        check_vma=False,
    )
```

```python
import jax
import jax.numpy as jnp
from jax import lax
from jax.sharding import PartitionSpec as P
from jax.experimental import pallas as pl
from jax.experimental.pallas import tpu as pltpu

BLOCK = 64
WIDE = 128
LEVELS = 5
SHARES = (8, 8)
f32 = jnp.float32
bf16 = jnp.bfloat16
MEG = 1024 * 1024
FINISH = 16
LOCAL = 62.25
PARTS = 1
SIDE = 4
GATHER = 8


def mxu(a, b):
    return lax.dot_general(a, b, (((1,), (0,)), ((), ())), preferred_element_type=f32)


def mxu_t(a, b):
    return lax.dot_general(a, b, (((1,), (1,)), ((), ())), preferred_element_type=f32)


def halves(x):
    hi = x.astype(bf16)
    return hi, (x - hi.astype(f32)).astype(bf16)


def together(live):
    while live:
        live = [g for g in live if next(g, g) is not g]


def repeat(count, body, unroll):
    while count % unroll:
        unroll -= 1

    def step(i, _):
        together([body(i * unroll + j) for j in range(unroll)])
        return 0

    lax.fori_loop(0, count // unroll, step, 0)


def split(heads, shares):
    counts = [heads * share // sum(shares) for share in shares]
    counts[-1] = heads - sum(counts[:-1])
    return [(sum(counts[:g]), n) for g, n in enumerate(counts)]


def aligned(index, size):
    return pl.ds(pl.multiple_of(index * size, size), size)


def left_half():
    return lax.broadcasted_iota(jnp.int32, (BLOCK, WIDE), 1) < BLOCK


def diagonal(x, left):
    zero = jnp.zeros_like(x)
    return jnp.concatenate([jnp.where(left, x, zero), jnp.where(left, zero, x)], axis=0)


def column(table, lane, at):
    picked = jnp.sum(jnp.where(lane == at, table, 0.0), axis=1, keepdims=True)
    return jnp.broadcast_to(picked, (BLOCK, WIDE))


def local_kernel(solve, span, heads, depth, levels_ref, *refs):
    first, count = span
    names = ["weight", "row", "col", "kn", "t", "q", "v"]
    if solve:
        names = ["weight", "ld", "wr", "k", "q", "v"]
    inputs, refs = dict(zip(names, refs)), refs[len(names):]
    run_ref, term_hbm, mark_ref, refs = *refs[:3], refs[3:]
    mark_ref[...] = jnp.zeros_like(mark_ref)
    if solve:
        row_s, colg_s, kn_hbm, t_hbm, refs = *refs[:4], refs[4:]
        ld_s, wr_s, k_s, low_s, inv_s, colb_s, key_sem, refs = *refs[:7], refs[7:]
    else:
        row_s, colg_s = inputs["row"], inputs["col"]
    (
        weight_s, q_s, v_s, kn_s, gram_s, scale_s, m_s, fall_s, s_s, qt_s, near_s, p_s, term_s, copy_sem,
        pair_sem, keep_sem, step_sem,
    ) = refs
    tokens = q_s.shape[0]
    pairs = tokens // WIDE
    units = heads * pairs
    blocks = tokens // BLOCK
    lanes = 2 * units
    across = heads if solve else count
    mine = slice(first * WIDE, (first + count) * WIDE)

    loads = {"weight": (inputs["weight"], weight_s)}
    if solve:
        loads.update(ld=(inputs["ld"], ld_s), wr=(inputs["wr"], wr_s))

    def pair_copies(p):
        toks = aligned(p, WIDE)
        copies = [
            (inputs["q"].at[toks, mine], q_s.at[toks, :]),
            (inputs["v"].at[toks, mine], v_s.at[toks, :]),
        ]
        if not solve:
            size = count * BLOCK
            at = pl.ds(pl.multiple_of((p * heads + first) * BLOCK, BLOCK), size)
            copies += [
                (inputs["kn"].at[first:first + count, toks, :], kn_s.at[:, toks, :]),
                (inputs["t"].at[at, :], gram_s.at[aligned(p, size), :]),
            ]
        return [
            pltpu.make_async_copy(x, y, pair_sem.at[p, i]) for i, (x, y) in enumerate(copies)
        ]

    if solve:
        for i, name in enumerate(("q", "v")):
            loads[name] = (inputs[name].at[:, mine], (q_s, v_s)[i])

    loads = {
        name: pltpu.make_async_copy(x, y, copy_sem.at[i])
        for i, (name, (x, y)) in enumerate(loads.items())
    }
    if solve:
        quarter = k_s.shape[1] // 4

        def key_copy(i):
            part = aligned(i, quarter)
            return pltpu.make_async_copy(inputs["k"].at[:, part], k_s.at[:, part], key_sem.at[i])

        loads["ld"].start()
        loads["wr"].start()
        for i in range(4):
            key_copy(i).start()
    if not solve:
        for p in range(pairs):
            for c in pair_copies(p):
                c.start()
    for name, c in loads.items():
        if name not in ("ld", "wr"):
            c.start()

    left = left_half()
    ri = lax.broadcasted_iota(jnp.int32, (WIDE, WIDE), 0)
    ci = lax.broadcasted_iota(jnp.int32, (WIDE, WIDE), 1)

    def inverses():
        tri = jnp.where((ri <= ci) & ((ri >= BLOCK) == (ci >= BLOCK)), 1.0, 0.0)
        def by_unit(x):
            return jnp.concatenate([x[:, p * WIDE:(p + 1) * WIDE] for p in range(pairs)], axis=0)

        loads["ld"].wait()
        loads["wr"].wait()
        grow = lax.dot_general(
            by_unit(ld_s[...]), tri, (((1,), (0,)), ((), ())),
            precision=lax.Precision.HIGHEST, preferred_element_type=f32,
        )
        row_s[...] = grow
        gcol = grow.T
        bcol = by_unit(wr_s[...]).T
        colg_s[...] = jnp.concatenate([gcol[:BLOCK], gcol[BLOCK:]], axis=1)
        colb_s[...] = jnp.concatenate([bcol[:BLOCK], bcol[BLOCK:]], axis=1)

        def keys(h):
            cols = aligned(h, WIDE)
            kf = k_s[:, cols].astype(f32)
            total = jnp.sum(kf * kf, axis=1, keepdims=True)
            yield
            kn = (kf * lax.rsqrt(total + 1e-6)).astype(bf16)
            kn_s[h] = kn
            grams = []
            for p in range(pairs):
                kp = kn[p * WIDE:(p + 1) * WIDE]
                grams.append(mxu_t(kp, kp))
            yield
            for p, g in enumerate(grams):
                gram_s[aligned(p * heads + h, BLOCK), :] = jnp.where(left, g[:BLOCK], g[BLOCK:])

        def key_group(i, _):
            key_copy(i).wait()
            together([keys(i * (heads // 4) + j) for j in range(heads // 4)])
            return 0

        lax.fori_loop(0, 4, key_group, 0)

        def to_lanes(i):
            a = gram_s[pl.ds(i, units, stride=BLOCK), :].T
            yield
            g = jnp.concatenate([a[:BLOCK], a[BLOCK:]], axis=1)
            gi = colg_s[pl.ds(i, 1), :]
            bi = colb_s[pl.ds(i, 1), :]
            e = jnp.exp(gi - colg_s[...])
            yield
            low_s[i] = g * (bi * e)
            inv_s[i] = jnp.zeros_like(g)

        repeat(BLOCK, to_lanes, 32)

        sub = lax.broadcasted_iota(jnp.int32, (8, lanes), 0)

        def solve(bi, _):
            i0 = bi * 8

            def columns(cb, _):
                c = aligned(cb, 8)

                def step(jb, acc):
                    acc = list(acc)
                    for jj in range(8):
                        j = jb * 8 + jj
                        t = inv_s[j, c, :]
                        for r in range(8):
                            acc[r] = acc[r] - low_s[i0 + r, pl.ds(j, 1), :] * t
                    return tuple(acc)

                on = cb == bi
                acc = tuple(jnp.where((sub == r) & on, 1.0, 0.0) for r in range(8))
                acc = list(lax.fori_loop(cb, bi, step, acc))
                for r in range(8):
                    inv_s[i0 + r, c, :] = acc[r]
                    for s in range(r + 1, 8):
                        acc[s] = acc[s] - low_s[i0 + s, pl.ds(i0 + r, 1), :] * acc[r]
                return 0

            lax.fori_loop(0, bi + 1, columns, 0)
            return 0

        lax.fori_loop(0, BLOCK // 8, solve, 0)

        def from_lanes(i):
            t = inv_s[i] * colb_s[...]
            a = jnp.concatenate([t[:, :units], t[:, units:]], axis=0).T
            yield
            gram_s[pl.ds(i, units, stride=BLOCK), :] = a

        repeat(BLOCK, from_lanes, 32)

    kept = []
    if solve:
        inverses()
        kept = [(kn_s, kn_hbm), (gram_s.at[:units * BLOCK], t_hbm)]
        kept = [pltpu.make_async_copy(x, y, keep_sem.at[i]) for i, (x, y) in enumerate(kept)]
        for c in kept:
            c.start()
    clane = lax.broadcasted_iota(jnp.int32, (BLOCK, lanes), 1)
    lane = lax.broadcasted_iota(jnp.int32, (BLOCK, WIDE), 1)
    row64 = lax.broadcasted_iota(jnp.int32, (BLOCK, WIDE), 0)
    keep = row64 >= jnp.where(left, lane, lane - BLOCK)
    eye = ri == ci

    def unit(p, h):
        i = p * count + h
        u = p * heads + first + h
        grow = row_s[pl.ds(u, 1), :]
        gs = [column(colg_s[...], clane, u), column(colg_s[...], clane, u + units)]
        kn = kn_s[h, aligned(p, WIDE), :]
        v = v_s[aligned(p, WIDE), aligned(h, WIDE)]
        q = q_s[aligned(p, WIDE), aligned(h, WIDE)]
        qk = mxu_t(q, kn)
        t1 = gram_s[aligned(p * across + h, BLOCK), :]
        t2 = t1 * jnp.exp(grow)
        a_hi, a_lo = halves(diagonal(t1, left))
        b_hi, b_lo = halves(diagonal(t2, left))
        wv = mxu(jnp.concatenate([a_hi, a_lo], axis=1), jnp.concatenate([v, v], axis=0))
        wk = mxu(jnp.concatenate([b_hi, b_lo], axis=1), jnp.concatenate([kn, kn], axis=0))
        knt = kn.astype(f32).T.astype(bf16)
        decay = jnp.exp(jnp.where(keep, jnp.where(left, gs[0], gs[1]) - grow, -1e30))
        yield
        score = diagonal(jnp.where(left, qk[:BLOCK], qk[BLOCK:]) * decay, left).astype(bf16)
        w = jnp.concatenate([wv, wk], axis=1)
        kk = jnp.concatenate([knt, knt], axis=1)
        outs = []
        for half, g in enumerate(gs):
            end = g[BLOCK - 1:, :]
            tail = jnp.exp(end - g)
            part = w[half * BLOCK:(half + 1) * BLOCK] * jnp.concatenate([tail, tail], axis=1)
            hi, lo = halves(part)
            none = jnp.zeros_like(hi)
            stack = [hi, none, lo, none] if half == 0 else [none, hi, none, lo]
            outs.append((end, mxu(kk, jnp.concatenate(stack, axis=0))))
        ys = mxu(score, w.astype(bf16))
        yield
        for half, (end, y) in enumerate(outs):
            s_s[2 * p + half, h] = y[:, :WIDE]
            m_s[2 * p + half, h] = y[:, WIDE:].astype(bf16)
            fall_s[2 * p + half, pl.ds(h, 1), :] = jnp.exp(end)
        near_s[i] = ys[:, :WIDE]
        eg = jnp.exp(jnp.concatenate(gs, axis=0))
        qt_s[i] = (eg * q.astype(f32) - ys[:, WIDE:]).astype(bf16)

    if solve:
        loads["q"].wait()
        loads["v"].wait()

    def pair_units(p, _):
        if not solve:
            for c in pair_copies(p):
                c.wait()
        repeat(count, lambda h: unit(p, h), 8)
        return 0

    lax.fori_loop(0, pairs, pair_units, 0)

    loads["weight"].wait()
    slots = weight_s.shape[0]
    level = lax.rem(lax.broadcasted_iota(jnp.int32, (BLOCK, slots), 1), LEVELS)
    weight = weight_s[...].T
    for b in range(blocks):
        toks = slice(b * BLOCK, (b + 1) * BLOCK)
        scale_s[toks, :] = jnp.where(level < levels_ref[b], weight[toks], 0.0)

    def term_copy(b):
        toks = aligned(b, BLOCK)
        return pltpu.make_async_copy(term_s.at[b], term_hbm.at[:, toks, :], step_sem.at[b])

    def write(b, h, near, rows):
        cols = pl.ds(h * WIDE, WIDE)
        scale = scale_s[aligned(b, BLOCK), :]
        for i in range(1 + depth):
            at = (first + h) * LEVELS + i
            term_s[b, i, :, cols] = ((rows if i else near) * scale[:, at:at + 1]).astype(bf16)

    for h in range(count):
        p_s[h, :, :WIDE] = s_s[0, h]
        p_s[h, :, WIDE:] = jnp.where(eye, fall_s[0, h:h + 1, :], 0.0) - m_s[0, h].astype(f32)
        write(0, h, near_s[h, :BLOCK, :], qt_s[h, :BLOCK, :].astype(f32))
    term_copy(0).start()

    def scan(b, _):
        half = aligned(b % 2, BLOCK)

        def advance(h):
            i = (b // 2) * count + h
            both = mxu(
                jnp.concatenate([m_s[b, h], qt_s[i, half, :]], axis=0), p_s[h].astype(bf16)
            )
            yield
            fall = fall_s[b, h:h + 1, :]
            n, o = both[:WIDE], both[WIDE:]
            p_s[h, :, :WIDE] = fall * p_s[h, :, :WIDE] + s_s[b, h] - n[:, :WIDE]
            p_s[h, :, WIDE:] = fall * p_s[h, :, WIDE:] - n[:, WIDE:]
            write(b, h, near_s[i, half, :] + o[:, :WIDE], o[:, WIDE:])

        for h in range(0, count, SIDE):
            together([advance(h + j) for j in range(min(SIDE, count - h))])
        term_copy(b).start()
        return 0

    lax.fori_loop(1, blocks, scan, 0)
    for h in range(count):
        run_ref[h] = p_s[h].astype(bf16)
    for c in kept:
        c.wait()
    for b in range(blocks):
        term_copy(b).wait()


def local_call(span, heads, depth, levels, weights, solved, inputs, q, v, after):
    tokens = q.shape[0]
    first, count = span
    pairs = tokens // WIDE
    units = heads * pairs
    blocks = tokens // BLOCK
    solve = solved is None
    smem = pl.BlockSpec(memory_space=pltpu.SMEM)
    vmem = pl.BlockSpec(memory_space=pltpu.VMEM)
    hbm = pl.BlockSpec(memory_space=pltpu.HBM)
    after, spaces = waits(after)
    out_specs = [vmem, hbm, vmem]
    out_shape = [
        jax.ShapeDtypeStruct((count, WIDE, 2 * WIDE), bf16),
        jax.ShapeDtypeStruct((1 + depth, tokens, count * WIDE), bf16),
        jax.ShapeDtypeStruct((8, WIDE), f32),
    ]
    scratch = []
    if solve:
        operands = [weights, *inputs, q, v]
        in_specs = [hbm] * 6
        out_specs += [vmem, vmem, hbm, hbm]
        out_shape += [
            jax.ShapeDtypeStruct((units, WIDE), f32),
            jax.ShapeDtypeStruct((BLOCK, 2 * units), f32),
            jax.ShapeDtypeStruct((heads, tokens, WIDE), bf16),
            jax.ShapeDtypeStruct((units * BLOCK, WIDE), f32),
        ]
        scratch = [
            pltpu.VMEM(inputs[0].shape, f32),
            pltpu.VMEM(inputs[1].shape, f32),
            pltpu.VMEM(inputs[2].shape, bf16),
            pltpu.VMEM((BLOCK, BLOCK, 2 * units), f32),
            pltpu.VMEM((BLOCK, BLOCK, 2 * units), f32),
            pltpu.VMEM((BLOCK, 2 * units), f32),
            pltpu.SemaphoreType.DMA((4,)),
        ]
    else:
        operands = [weights, *solved, q, v]
        in_specs = [hbm, vmem, vmem, hbm, hbm, hbm, hbm]
    across = heads if solve else count

    def kernel(*refs):
        used = 1 + len(operands)
        local_kernel(solve, span, heads, depth, *refs[:used], *refs[used + len(after):])

    return pl.pallas_call(
        kernel,
        in_specs=[smem] + in_specs + spaces,
        out_specs=out_specs,
        out_shape=out_shape,
        scratch_shapes=scratch
        + [
            pltpu.VMEM(weights.shape, f32),
            pltpu.VMEM((tokens, count * WIDE), bf16),
            pltpu.VMEM((tokens, count * WIDE), bf16),
            pltpu.VMEM((across, tokens, WIDE), bf16),
            pltpu.VMEM((across * pairs * BLOCK + (BLOCK if solve else 0), WIDE), f32),
            pltpu.VMEM((tokens, weights.shape[0]), f32),
            pltpu.VMEM((blocks, count, WIDE, WIDE), bf16),
            pltpu.VMEM((blocks, count, WIDE), f32),
            pltpu.VMEM((blocks, count, WIDE, WIDE), f32),
            pltpu.VMEM((pairs * count, WIDE, WIDE), bf16),
            pltpu.VMEM((pairs * count, WIDE, WIDE), f32),
            pltpu.VMEM((count, WIDE, 2 * WIDE), f32),
            pltpu.VMEM((blocks, 1 + depth, BLOCK, count * WIDE), bf16),
            pltpu.SemaphoreType.DMA((5,)),
            pltpu.SemaphoreType.DMA((pairs, 4)),
            pltpu.SemaphoreType.DMA((2,)),
            pltpu.SemaphoreType.DMA((blocks,)),
        ],
        compiler_params=pltpu.CompilerParams(vmem_limit_bytes=int(LOCAL * MEG)),
        name="local",
    )(levels, *operands, *after)


def waits(after):
    return [x for x, _ in after], [pl.BlockSpec(memory_space=space) for _, space in after]


def pair_kernel(flag_ref, own_ref, other_ref, *rest):
    s_ref, m_ref = rest[-2:]
    heads = own_ref.shape[0]
    upper = flag_ref[0] == 1

    def head(h):
        own = own_ref[h]
        other = other_ref[h]
        late = jnp.where(upper, own, other)
        early = jnp.where(upper, other, own)
        both = mxu(late[:, WIDE:], early)
        yield
        s_ref[h] = (both[:, :WIDE] + late[:, :WIDE].astype(f32)).astype(bf16)
        m_ref[h] = both[:, WIDE:].astype(bf16)

    together([head(h) for h in range(heads)])


def pair_call(flag, own, other, after):
    square = jax.ShapeDtypeStruct((own.shape[0], WIDE, WIDE), bf16)
    vmem = pl.BlockSpec(memory_space=pltpu.VMEM)
    after, spaces = waits(after)
    return pl.pallas_call(
        pair_kernel,
        in_specs=[pl.BlockSpec(memory_space=pltpu.SMEM), vmem, vmem]
        + spaces,
        out_specs=[vmem, vmem],
        out_shape=[square, square],
        compiler_params=pltpu.CompilerParams(vmem_limit_bytes=8 * MEG),
        name="pair",
    )(flag, own, other, *after)


def hop_kernel(m_ref, *refs):
    *entry_refs, out_ref = refs

    def head(h):
        entry = entry_refs[1][h]
        for ref in entry_refs[2:]:
            entry = (entry.astype(f32) + ref[h].astype(f32)).astype(bf16)
        o = mxu(m_ref[h], entry)
        yield
        if entry_refs[0] is not None:
            o = o + entry_refs[0][h].astype(f32)
        out_ref[h] = o.astype(bf16)

    together([head(h) for h in range(m_ref.shape[0])])


def hop_call(m, s, entries, after):
    vmem = pl.BlockSpec(memory_space=pltpu.VMEM)
    operands = ([] if s is None else [s]) + entries

    after, spaces = waits(after)

    def kernel(m_ref, *refs):
        used = refs[:len(operands)] + refs[-1:]
        hop_kernel(m_ref, *(used if s is not None else (None,) + used))

    return pl.pallas_call(
        kernel,
        in_specs=[vmem] * (1 + len(operands)) + spaces,
        out_specs=vmem,
        out_shape=jax.ShapeDtypeStruct(m.shape, bf16),
        compiler_params=pltpu.CompilerParams(vmem_limit_bytes=8 * MEG),
        name="hop",
    )(m, *operands, *after)


def stage_kernel(from_ref, *refs):
    refs[-1][...] = from_ref[...]


def stage_call(terms, after):
    vmem = pl.BlockSpec(memory_space=pltpu.VMEM)
    after, spaces = waits(after)
    return pl.pallas_call(
        stage_kernel,
        in_specs=[vmem] + spaces,
        out_specs=vmem,
        out_shape=jax.ShapeDtypeStruct(terms.shape, terms.dtype),
        compiler_params=pltpu.CompilerParams(vmem_limit_bytes=16 * MEG),
        name="stage",
    )(terms, *after)


def finish_kernel(span, size, shape, here_ref, term_ref, other_ref, *refs):
    entries, at = [], 0
    for count in shape:
        entries.append(refs[at:at + count])
        at += count
    outs = refs[at:at + size]
    depth, tokens, width = term_ref.shape
    chunk = tokens // size
    heads = range(span[0], sum(span))
    here = here_ref[0]
    position = here_ref[1]
    zero = jnp.zeros((WIDE, WIDE), bf16)
    odd = (position & 1) == 1
    pair = position >> 1
    carries = []
    for h in heads:
        came = []
        for m, options in enumerate(entries):
            entry = zero
            for j, ref in enumerate(options):
                mine = ((pair >> m) & 1 == 1) & ((pair & ((1 << m) - 1)) == j)
                entry = jnp.where(mine, ref[h], entry)
            came.append(entry)
        wide = jnp.concatenate(came, axis=1)
        ahead = mxu(other_ref[h, :, WIDE:], wide).astype(bf16)
        carries.append(jnp.concatenate(
            [jnp.where(odd, other_ref[h, :, :WIDE], zero)]
            + [
                jnp.where(odd, ahead[:, m * WIDE:(m + 1) * WIDE], x) for m, x in enumerate(came)
            ],
            axis=0,
        ))
    for d in range(size):
        toks = aligned(here ^ d, chunk)

        def head(h):
            part = slice(h * WIDE, (h + 1) * WIDE)
            far = jnp.concatenate([term_ref[i, toks, part] for i in range(1, depth)], axis=1)
            total = mxu(far, carries[h - span[0]])
            yield
            out = slice((h - span[0]) * WIDE, (h - span[0] + 1) * WIDE)
            outs[d][:, out] = (total + term_ref[0, toks, part].astype(f32)).astype(bf16)

        together([head(h) for h in heads])


def finish_call(span, size, here, terms, other, entries, after):
    depth, tokens, width = terms.shape
    smem = pl.BlockSpec(memory_space=pltpu.SMEM)
    vmem = pl.BlockSpec(memory_space=pltpu.VMEM)
    shape = [len(e) for e in entries]
    flat = [x for e in entries for x in e]
    after, spaces = waits(after)

    def kernel(*refs):
        used = 3 + len(flat)
        finish_kernel(span, size, shape, *refs[:used], *refs[used + len(after):])

    return pl.pallas_call(
        kernel,
        in_specs=[smem] + [vmem] * (2 + len(flat)) + spaces,
        out_specs=[vmem] * size,
        out_shape=[jax.ShapeDtypeStruct((tokens // size, span[1] * WIDE), bf16)] * size,
        compiler_params=pltpu.CompilerParams(vmem_limit_bytes=FINISH * MEG),
        name="finish",
    )(here, terms, other, *flat, *after)


def gather_kernel(first, heads, sources, place_ref, *refs):
    parts, (out_ref, mark_ref, sems) = refs[:len(sources)], refs[-3:]
    mark_ref[...] = jnp.zeros_like(mark_ref)
    here = place_ref[0]
    copies = []
    for i, (d, ref) in enumerate(zip(sources, parts)):
        col = pl.multiple_of(((here ^ d) * heads + first) * WIDE, WIDE)
        where = out_ref.at[:, pl.ds(col, ref.shape[1])]
        copies.append(pltpu.make_async_copy(ref, where, sems.at[i]))
        copies[-1].start()
    for c in copies:
        c.wait()


def gather_call(first, heads, size, place, parts, before, after):
    sources, parts = zip(*parts)
    count = len(parts)
    vmem = pl.BlockSpec(memory_space=pltpu.VMEM)
    hbm = pl.BlockSpec(memory_space=pltpu.HBM)
    after, spaces = waits(after)
    kept = [] if before is None else [before]

    def kernel(*refs):
        gather_kernel(first, heads, sources, *refs)

    return pl.pallas_call(
        kernel,
        in_specs=[pl.BlockSpec(memory_space=pltpu.SMEM)] + [vmem] * count + [hbm] * len(kept)
        + spaces,
        out_specs=[hbm, vmem],
        out_shape=[
            jax.ShapeDtypeStruct((parts[0].shape[0], heads * size * WIDE), bf16),
            jax.ShapeDtypeStruct((8, WIDE), f32),
        ],
        input_output_aliases={1 + count: 0} if kept else {},
        scratch_shapes=[pltpu.SemaphoreType.DMA((count,))],
        compiler_params=pltpu.CompilerParams(vmem_limit_bytes=GATHER * MEG),
        name="gather",
    )(place, *parts, *kept, *after)


ORDER = ("l0", "l1", "p0", "h01", "p1", "h02", "h11", "t0", "f00")
ORDER += ("h12", "t1", "a00", "f10", "b00", "a10", "b10")


def order(groups, steps):
    names = dict(l="local", p="pair", t="stage", h="hop", f="finish", g="gather", a="some", b="rest")
    if steps == 3:
        return [(names[x[0]], int(x[1]), int(x[2:] or 0)) for x in ORDER]
    out = [("local", g, 0) for g in range(groups)] + [("pair", g, 0) for g in range(groups)]
    out += [("hop", g, step) for step in range(1, steps) for g in range(groups)]
    out += [("finish", g, i) for g in range(groups) for i in range(PARTS)]
    return out + [("gather", g, i) for g in range(groups) for i in range(PARTS)]


def per_device(queries, key_rows, value_rows, log_decay, write_rate, level_weights, block_levels):
    size = lax.axis_size("ctx")
    bits = size.bit_length() - 1
    width = lax.axis_size("head")
    position = lax.axis_index("ctx").astype(jnp.int32)
    place = lax.axis_index("head").astype(jnp.int32)
    here = jnp.stack([place, position])
    flag = (position & 1).reshape(1)
    heads = log_decay.shape[1]
    groups = split(heads, SHARES)
    pairs = size // 2
    steps = [(m, j) for m in range(pairs.bit_length() - 1) for j in range(1 << m)]

    def swap(low, array):
        to = list(range(pairs))
        for p in low:
            to[p], to[p + 1] = p + 1, p
        return lax.ppermute(array, "ctx", [(i, 2 * to[i >> 1] + (i & 1)) for i in range(size)])

    runs, others, terms, states, solved = {}, {}, {}, {}, []
    entries = [[] for _ in groups]
    pieces = {}
    after = []

    def local(g):
        runs[g], terms[g], mark, *kept = local_call(
            groups[g], heads, bits, block_levels, level_weights.T, solved[0] if solved else None,
            [log_decay.T, write_rate.T, key_rows], queries, value_rows, after,
        )
        if kept:
            solved.append(kept)
        others[g] = lax.ppermute(runs[g], "ctx", [(i, i ^ 1) for i in range(size)])
        return mark, pltpu.VMEM

    def pair(g):
        states[g] = pair_call(flag, runs[g], others[g], after)
        return states[g][1], pltpu.VMEM

    def hop(g, step):
        m, j = steps[step]
        s, t = states[g]
        if j:
            sent = hop_call(t, None, [entries[g][m][j - 1]], after)
        elif m:
            sent = hop_call(t, s, [e[-1] for e in entries[g]], after)
        else:
            sent = s
        if j == 0:
            entries[g].append([])
        low = [p for p in range(pairs) if p % (2 << m) == (1 << m) + j - 1]
        entries[g][m].append(swap(low, sent))
        return sent, pltpu.VMEM

    def stage(g):
        terms[g] = stage_call(terms[g], after)
        return terms[g], pltpu.VMEM

    def span_of(g, part):
        return split(groups[g][1], (1,) * PARTS)[part]

    def finish(g, part):
        outs = finish_call(
            span_of(g, part), width, here, terms[g], others[g], entries[g], after
        )
        for d in range(width):
            pairing = [(i, i ^ d) for i in range(width)]
            pieces[g, part, d] = outs[d] if d == 0 else lax.ppermute(outs[d], "head", pairing)
        return outs[0], pltpu.VMEM

    def gather(g, part, out, ds):
        parts = [(d, pieces[g, part, d]) for d in ds]
        first = groups[g][0] + span_of(g, part)[0]
        return gather_call(first, heads, width, place.reshape(1), parts, out, after)

    out = None
    for name, g, step in order(len(groups), len(steps)):
        if name == "local":
            token = local(g)
        elif name == "pair":
            token = pair(g)
            hop(g, 0)
        elif name == "stage":
            token = stage(g)
        elif name == "hop":
            token = hop(g, step)
        elif name == "finish":
            token = finish(g, step)
        else:
            cut = width - 1
            ds = dict(some=range(cut), rest=range(cut, width)).get(name, range(width))
            out, mark = gather(g, step, out, ds)
            token = mark, pltpu.VMEM
        after = [token]
    return out


def solution(mesh):
    wide = P("ctx", "head")
    return jax.shard_map(
        per_device,
        mesh=mesh,
        in_specs=(wide, wide, wide, wide, wide, wide, P("ctx")),
        out_specs=P(("ctx", "head"), None),
        check_vma=False,
    )
```

```python
import jax
import jax.numpy as jnp
from jax import lax
from jax.sharding import PartitionSpec as P
from jax.experimental import pallas as pl
from jax.experimental.pallas import tpu as pltpu

BLOCK = 64
WIDE = 128
LEVELS = 5
SHARES = (8, 8)
f32 = jnp.float32
bf16 = jnp.bfloat16
MEG = 1024 * 1024
FINISH = 16
LOCAL = 62.25
PARTS = 1
SIDE = 4
GATHER = 8


def mxu(a, b):
    return lax.dot_general(a, b, (((1,), (0,)), ((), ())), preferred_element_type=f32)


def mxu_t(a, b):
    return lax.dot_general(a, b, (((1,), (1,)), ((), ())), preferred_element_type=f32)


def halves(x):
    hi = x.astype(bf16)
    return hi, (x - hi.astype(f32)).astype(bf16)


def together(live):
    while live:
        live = [g for g in live if next(g, g) is not g]


def repeat(count, body, unroll):
    while count % unroll:
        unroll -= 1

    def step(i, _):
        together([body(i * unroll + j) for j in range(unroll)])
        return 0

    lax.fori_loop(0, count // unroll, step, 0)


def split(heads, shares):
    counts = [heads * share // sum(shares) for share in shares]
    counts[-1] = heads - sum(counts[:-1])
    return [(sum(counts[:g]), n) for g, n in enumerate(counts)]


def aligned(index, size):
    return pl.ds(pl.multiple_of(index * size, size), size)


def left_half():
    return lax.broadcasted_iota(jnp.int32, (BLOCK, WIDE), 1) < BLOCK


def diagonal(x, left):
    zero = jnp.zeros_like(x)
    return jnp.concatenate([jnp.where(left, x, zero), jnp.where(left, zero, x)], axis=0)


def column(table, lane, at):
    picked = jnp.sum(jnp.where(lane == at, table, 0.0), axis=1, keepdims=True)
    return jnp.broadcast_to(picked, (BLOCK, WIDE))


def local_kernel(solve, span, heads, depth, levels_ref, *refs):
    first, count = span
    names = ["weight", "row", "col", "kn", "t", "q", "v"]
    if solve:
        names = ["weight", "ld", "wr", "k", "q", "v"]
    inputs, refs = dict(zip(names, refs)), refs[len(names):]
    run_ref, term_hbm, mark_ref, refs = *refs[:3], refs[3:]
    mark_ref[...] = jnp.zeros_like(mark_ref)
    if solve:
        row_s, colg_s, kn_hbm, t_hbm, refs = *refs[:4], refs[4:]
        ld_s, wr_s, k_s, low_s, inv_s, colb_s, key_sem, refs = *refs[:7], refs[7:]
    else:
        row_s, colg_s = inputs["row"], inputs["col"]
    (
        weight_s, q_s, v_s, kn_s, gram_s, scale_s, m_s, fall_s, s_s, qt_s, near_s, p_s, term_s, run_s, copy_sem,
        pair_sem, keep_sem, step_sem,
    ) = refs
    tokens = q_s.shape[0]
    pairs = tokens // WIDE
    units = heads * pairs
    blocks = tokens // BLOCK
    lanes = 2 * units
    across = heads if solve else count
    mine = slice(first * WIDE, (first + count) * WIDE)

    loads = {"weight": (inputs["weight"], weight_s)}
    if solve:
        loads.update(ld=(inputs["ld"], ld_s), wr=(inputs["wr"], wr_s))

    def pair_copies(p):
        toks = aligned(p, WIDE)
        copies = [
            (inputs["q"].at[toks, mine], q_s.at[toks, :]),
            (inputs["v"].at[toks, mine], v_s.at[toks, :]),
        ]
        if not solve:
            size = count * BLOCK
            at = pl.ds(pl.multiple_of((p * heads + first) * BLOCK, BLOCK), size)
            copies += [
                (inputs["kn"].at[first:first + count, toks, :], kn_s.at[:, toks, :]),
                (inputs["t"].at[at, :], gram_s.at[aligned(p, size), :]),
            ]
        return [
            pltpu.make_async_copy(x, y, pair_sem.at[p, i]) for i, (x, y) in enumerate(copies)
        ]

    if solve:
        for i, name in enumerate(("q", "v")):
            loads[name] = (inputs[name].at[:, mine], (q_s, v_s)[i])

    loads = {
        name: pltpu.make_async_copy(x, y, copy_sem.at[i])
        for i, (name, (x, y)) in enumerate(loads.items())
    }
    if solve:
        quarter = k_s.shape[1] // 4

        def key_copy(i):
            part = aligned(i, quarter)
            return pltpu.make_async_copy(inputs["k"].at[:, part], k_s.at[:, part], key_sem.at[i])

        loads["ld"].start()
        loads["wr"].start()
        for i in range(4):
            key_copy(i).start()
    if not solve:
        for p in range(pairs):
            for c in pair_copies(p):
                c.start()
    for name, c in loads.items():
        if name not in ("ld", "wr"):
            c.start()

    left = left_half()
    ri = lax.broadcasted_iota(jnp.int32, (WIDE, WIDE), 0)
    ci = lax.broadcasted_iota(jnp.int32, (WIDE, WIDE), 1)

    def inverses():
        tri = jnp.where((ri <= ci) & ((ri >= BLOCK) == (ci >= BLOCK)), 1.0, 0.0)
        def by_unit(x):
            return jnp.concatenate([x[:, p * WIDE:(p + 1) * WIDE] for p in range(pairs)], axis=0)

        loads["ld"].wait()
        loads["wr"].wait()
        grow = lax.dot_general(
            by_unit(ld_s[...]), tri, (((1,), (0,)), ((), ())),
            precision=lax.Precision.HIGHEST, preferred_element_type=f32,
        )
        row_s[...] = grow
        gcol = grow.T
        bcol = by_unit(wr_s[...]).T
        colg_s[...] = jnp.concatenate([gcol[:BLOCK], gcol[BLOCK:]], axis=1)
        colb_s[...] = jnp.concatenate([bcol[:BLOCK], bcol[BLOCK:]], axis=1)

        def keys(h):
            cols = aligned(h, WIDE)
            kf = k_s[:, cols].astype(f32)
            total = jnp.sum(kf * kf, axis=1, keepdims=True)
            yield
            kn = (kf * lax.rsqrt(total + 1e-6)).astype(bf16)
            kn_s[h] = kn
            grams = []
            for p in range(pairs):
                kp = kn[p * WIDE:(p + 1) * WIDE]
                grams.append(mxu_t(kp, kp))
            yield
            for p, g in enumerate(grams):
                gram_s[aligned(p * heads + h, BLOCK), :] = jnp.where(left, g[:BLOCK], g[BLOCK:])

        def key_group(i, _):
            key_copy(i).wait()
            together([keys(i * (heads // 4) + j) for j in range(heads // 4)])
            return 0

        lax.fori_loop(0, 4, key_group, 0)

        def to_lanes(i):
            a = gram_s[pl.ds(i, units, stride=BLOCK), :].T
            yield
            g = jnp.concatenate([a[:BLOCK], a[BLOCK:]], axis=1)
            gi = colg_s[pl.ds(i, 1), :]
            bi = colb_s[pl.ds(i, 1), :]
            e = jnp.exp(gi - colg_s[...])
            yield
            low_s[i] = g * (bi * e)
            inv_s[i] = jnp.zeros_like(g)

        repeat(BLOCK, to_lanes, 32)

        sub = lax.broadcasted_iota(jnp.int32, (8, lanes), 0)

        def solve(bi, _):
            i0 = bi * 8

            def columns(cb, _):
                c = aligned(cb, 8)

                def step(jb, acc):
                    acc = list(acc)
                    for jj in range(8):
                        j = jb * 8 + jj
                        t = inv_s[j, c, :]
                        for r in range(8):
                            acc[r] = acc[r] - low_s[i0 + r, pl.ds(j, 1), :] * t
                    return tuple(acc)

                on = cb == bi
                acc = tuple(jnp.where((sub == r) & on, 1.0, 0.0) for r in range(8))
                acc = list(lax.fori_loop(cb, bi, step, acc))
                for r in range(8):
                    inv_s[i0 + r, c, :] = acc[r]
                    for s in range(r + 1, 8):
                        acc[s] = acc[s] - low_s[i0 + s, pl.ds(i0 + r, 1), :] * acc[r]
                return 0

            lax.fori_loop(0, bi + 1, columns, 0)
            return 0

        lax.fori_loop(0, BLOCK // 8, solve, 0)

        def from_lanes(i):
            t = inv_s[i] * colb_s[...]
            a = jnp.concatenate([t[:, :units], t[:, units:]], axis=0).T
            yield
            gram_s[pl.ds(i, units, stride=BLOCK), :] = a

        repeat(BLOCK, from_lanes, 32)

    kept = []
    if solve:
        inverses()
        kept = [(kn_s, kn_hbm), (gram_s.at[:units * BLOCK], t_hbm)]
        kept = [pltpu.make_async_copy(x, y, keep_sem.at[i]) for i, (x, y) in enumerate(kept)]
        for c in kept:
            c.start()
    clane = lax.broadcasted_iota(jnp.int32, (BLOCK, lanes), 1)
    lane = lax.broadcasted_iota(jnp.int32, (BLOCK, WIDE), 1)
    row64 = lax.broadcasted_iota(jnp.int32, (BLOCK, WIDE), 0)
    keep = row64 >= jnp.where(left, lane, lane - BLOCK)
    eye = ri == ci

    def unit(p, h):
        i = p * count + h
        u = p * heads + first + h
        grow = row_s[pl.ds(u, 1), :]
        gs = [column(colg_s[...], clane, u), column(colg_s[...], clane, u + units)]
        kn = kn_s[h, aligned(p, WIDE), :]
        v = v_s[aligned(p, WIDE), aligned(h, WIDE)]
        q = q_s[aligned(p, WIDE), aligned(h, WIDE)]
        qk = mxu_t(q, kn)
        t1 = gram_s[aligned(p * across + h, BLOCK), :]
        t2 = t1 * jnp.exp(grow)
        a_hi, a_lo = halves(diagonal(t1, left))
        b_hi, b_lo = halves(diagonal(t2, left))
        wv = mxu(jnp.concatenate([a_hi, a_lo], axis=1), jnp.concatenate([v, v], axis=0))
        wk = mxu(jnp.concatenate([b_hi, b_lo], axis=1), jnp.concatenate([kn, kn], axis=0))
        knt = kn.astype(f32).T.astype(bf16)
        decay = jnp.exp(jnp.where(keep, jnp.where(left, gs[0], gs[1]) - grow, -1e30))
        yield
        score = diagonal(jnp.where(left, qk[:BLOCK], qk[BLOCK:]) * decay, left).astype(bf16)
        w = jnp.concatenate([wv, wk], axis=1)
        kk = jnp.concatenate([knt, knt], axis=1)
        outs = []
        for half, g in enumerate(gs):
            end = g[BLOCK - 1:, :]
            tail = jnp.exp(end - g)
            part = w[half * BLOCK:(half + 1) * BLOCK] * jnp.concatenate([tail, tail], axis=1)
            hi, lo = halves(part)
            none = jnp.zeros_like(hi)
            stack = [hi, none, lo, none] if half == 0 else [none, hi, none, lo]
            outs.append((end, mxu(kk, jnp.concatenate(stack, axis=0))))
        ys = mxu(score, w.astype(bf16))
        yield
        for half, (end, y) in enumerate(outs):
            s_s[2 * p + half, h] = y[:, :WIDE]
            m_s[2 * p + half, h] = y[:, WIDE:].astype(bf16)
            fall_s[2 * p + half, pl.ds(h, 1), :] = jnp.exp(end)
        near_s[i] = ys[:, :WIDE]
        eg = jnp.exp(jnp.concatenate(gs, axis=0))
        qt_s[i] = (eg * q.astype(f32) - ys[:, WIDE:]).astype(bf16)

    if solve:
        loads["q"].wait()
        loads["v"].wait()

    def pair_units(p, _):
        if not solve:
            for c in pair_copies(p):
                c.wait()
        repeat(count, lambda h: unit(p, h), 8)
        return 0

    lax.fori_loop(0, pairs, pair_units, 0)

    loads["weight"].wait()
    slots = weight_s.shape[0]
    level = lax.rem(lax.broadcasted_iota(jnp.int32, (BLOCK, slots), 1), LEVELS)
    weight = weight_s[...].T
    for b in range(blocks):
        toks = slice(b * BLOCK, (b + 1) * BLOCK)
        scale_s[toks, :] = jnp.where(level < levels_ref[b], weight[toks], 0.0)

    def term_copy(b):
        toks = aligned(b, BLOCK)
        return pltpu.make_async_copy(term_s.at[b], term_hbm.at[:, toks, :], step_sem.at[b])

    def write(b, h, near, rows):
        cols = pl.ds(h * WIDE, WIDE)
        scale = scale_s[aligned(b, BLOCK), :]
        for i in range(1 + depth):
            at = (first + h) * LEVELS + i
            term_s[b, i, :, cols] = ((rows if i else near) * scale[:, at:at + 1]).astype(bf16)

    for h in range(count):
        p_s[h, :, :WIDE] = s_s[0, h]
        p_s[h, :, WIDE:] = jnp.where(eye, fall_s[0, h:h + 1, :], 0.0) - m_s[0, h].astype(f32)
        write(0, h, near_s[h, :BLOCK, :], qt_s[h, :BLOCK, :].astype(f32))
    term_copy(0).start()

    def scan(b, _):
        half = aligned(b % 2, BLOCK)

        def advance(h):
            i = (b // 2) * count + h
            both = mxu(
                jnp.concatenate([m_s[b, h], qt_s[i, half, :]], axis=0), p_s[h].astype(bf16)
            )
            yield
            fall = fall_s[b, h:h + 1, :]
            n, o = both[:WIDE], both[WIDE:]
            p_s[h, :, :WIDE] = fall * p_s[h, :, :WIDE] + s_s[b, h] - n[:, :WIDE]
            p_s[h, :, WIDE:] = fall * p_s[h, :, WIDE:] - n[:, WIDE:]
            write(b, h, near_s[i, half, :] + o[:, :WIDE], o[:, WIDE:])

        for h in range(0, count, SIDE):
            together([advance(h + j) for j in range(min(SIDE, count - h))])
        term_copy(b).start()
        return 0

    lax.fori_loop(1, blocks, scan, 0)
    for h in range(count):
        run_s[h] = p_s[h].astype(bf16)
    run_copy = pltpu.make_async_copy(run_s, run_ref, keep_sem.at[2])
    run_copy.start()
    for c in kept:
        c.wait()
    for b in range(blocks):
        term_copy(b).wait()
    run_copy.wait()


def local_call(span, heads, depth, levels, weights, solved, inputs, q, v, after):
    tokens = q.shape[0]
    first, count = span
    pairs = tokens // WIDE
    units = heads * pairs
    blocks = tokens // BLOCK
    solve = solved is None
    smem = pl.BlockSpec(memory_space=pltpu.SMEM)
    vmem = pl.BlockSpec(memory_space=pltpu.VMEM)
    hbm = pl.BlockSpec(memory_space=pltpu.HBM)
    after, spaces = waits(after)
    out_specs = [hbm, hbm, vmem]
    out_shape = [
        jax.ShapeDtypeStruct((count, WIDE, 2 * WIDE), bf16),
        jax.ShapeDtypeStruct((1 + depth, tokens, count * WIDE), bf16),
        jax.ShapeDtypeStruct((8, WIDE), f32),
    ]
    scratch = []
    if solve:
        operands = [weights, *inputs, q, v]
        in_specs = [hbm] * 6
        out_specs += [vmem, vmem, hbm, hbm]
        out_shape += [
            jax.ShapeDtypeStruct((units, WIDE), f32),
            jax.ShapeDtypeStruct((BLOCK, 2 * units), f32),
            jax.ShapeDtypeStruct((heads, tokens, WIDE), bf16),
            jax.ShapeDtypeStruct((units * BLOCK, WIDE), f32),
        ]
        scratch = [
            pltpu.VMEM(inputs[0].shape, f32),
            pltpu.VMEM(inputs[1].shape, f32),
            pltpu.VMEM(inputs[2].shape, bf16),
            pltpu.VMEM((BLOCK, BLOCK, 2 * units), f32),
            pltpu.VMEM((BLOCK, BLOCK, 2 * units), f32),
            pltpu.VMEM((BLOCK, 2 * units), f32),
            pltpu.SemaphoreType.DMA((4,)),
        ]
    else:
        operands = [weights, *solved, q, v]
        in_specs = [hbm, vmem, vmem, hbm, hbm, hbm, hbm]
    across = heads if solve else count

    def kernel(*refs):
        used = 1 + len(operands)
        local_kernel(solve, span, heads, depth, *refs[:used], *refs[used + len(after):])

    return pl.pallas_call(
        kernel,
        in_specs=[smem] + in_specs + spaces,
        out_specs=out_specs,
        out_shape=out_shape,
        scratch_shapes=scratch
        + [
            pltpu.VMEM(weights.shape, f32),
            pltpu.VMEM((tokens, count * WIDE), bf16),
            pltpu.VMEM((tokens, count * WIDE), bf16),
            pltpu.VMEM((across, tokens, WIDE), bf16),
            pltpu.VMEM((across * pairs * BLOCK + (BLOCK if solve else 0), WIDE), f32),
            pltpu.VMEM((tokens, weights.shape[0]), f32),
            pltpu.VMEM((blocks, count, WIDE, WIDE), bf16),
            pltpu.VMEM((blocks, count, WIDE), f32),
            pltpu.VMEM((blocks, count, WIDE, WIDE), f32),
            pltpu.VMEM((pairs * count, WIDE, WIDE), bf16),
            pltpu.VMEM((pairs * count, WIDE, WIDE), f32),
            pltpu.VMEM((count, WIDE, 2 * WIDE), f32),
            pltpu.VMEM((blocks, 1 + depth, BLOCK, count * WIDE), bf16),
            pltpu.VMEM((count, WIDE, 2 * WIDE), bf16),
            pltpu.SemaphoreType.DMA((5,)),
            pltpu.SemaphoreType.DMA((pairs, 4)),
            pltpu.SemaphoreType.DMA((3,)),
            pltpu.SemaphoreType.DMA((blocks,)),
        ],
        compiler_params=pltpu.CompilerParams(vmem_limit_bytes=int(LOCAL * MEG)),
        name="local",
    )(levels, *operands, *after)


def waits(after):
    return [x for x, _ in after], [pl.BlockSpec(memory_space=space) for _, space in after]


def pair_kernel(flag_ref, own_ref, other_ref, *rest):
    s_ref, m_ref = rest[-2:]
    heads = own_ref.shape[0]
    upper = flag_ref[0] == 1

    def head(h):
        own = own_ref[h]
        other = other_ref[h]
        late = jnp.where(upper, own, other)
        early = jnp.where(upper, other, own)
        both = mxu(late[:, WIDE:], early)
        yield
        s_ref[h] = (both[:, :WIDE] + late[:, :WIDE].astype(f32)).astype(bf16)
        m_ref[h] = both[:, WIDE:].astype(bf16)

    together([head(h) for h in range(heads)])


def pair_call(flag, own, other, after):
    square = jax.ShapeDtypeStruct((own.shape[0], WIDE, WIDE), bf16)
    vmem = pl.BlockSpec(memory_space=pltpu.VMEM)
    after, spaces = waits(after)
    return pl.pallas_call(
        pair_kernel,
        in_specs=[pl.BlockSpec(memory_space=pltpu.SMEM), vmem, vmem]
        + spaces,
        out_specs=[vmem, vmem],
        out_shape=[square, square],
        compiler_params=pltpu.CompilerParams(vmem_limit_bytes=8 * MEG),
        name="pair",
    )(flag, own, other, *after)


def hop_kernel(m_ref, *refs):
    *entry_refs, out_ref = refs

    def head(h):
        entry = entry_refs[1][h]
        for ref in entry_refs[2:]:
            entry = (entry.astype(f32) + ref[h].astype(f32)).astype(bf16)
        o = mxu(m_ref[h], entry)
        yield
        if entry_refs[0] is not None:
            o = o + entry_refs[0][h].astype(f32)
        out_ref[h] = o.astype(bf16)

    together([head(h) for h in range(m_ref.shape[0])])


def hop_call(m, s, entries, after):
    vmem = pl.BlockSpec(memory_space=pltpu.VMEM)
    operands = ([] if s is None else [s]) + entries

    after, spaces = waits(after)

    def kernel(m_ref, *refs):
        used = refs[:len(operands)] + refs[-1:]
        hop_kernel(m_ref, *(used if s is not None else (None,) + used))

    return pl.pallas_call(
        kernel,
        in_specs=[vmem] * (1 + len(operands)) + spaces,
        out_specs=vmem,
        out_shape=jax.ShapeDtypeStruct(m.shape, bf16),
        compiler_params=pltpu.CompilerParams(vmem_limit_bytes=8 * MEG),
        name="hop",
    )(m, *operands, *after)


def stage_kernel(from_ref, *refs):
    refs[-1][...] = from_ref[...]


def stage_call(terms, after):
    vmem = pl.BlockSpec(memory_space=pltpu.VMEM)
    after, spaces = waits(after)
    return pl.pallas_call(
        stage_kernel,
        in_specs=[vmem] + spaces,
        out_specs=vmem,
        out_shape=jax.ShapeDtypeStruct(terms.shape, terms.dtype),
        compiler_params=pltpu.CompilerParams(vmem_limit_bytes=16 * MEG),
        name="stage",
    )(terms, *after)


def finish_kernel(span, size, shape, here_ref, term_ref, other_ref, *refs):
    entries, at = [], 0
    for count in shape:
        entries.append(refs[at:at + count])
        at += count
    outs = refs[at:at + size]
    depth, tokens, width = term_ref.shape
    chunk = tokens // size
    heads = range(span[0], sum(span))
    here = here_ref[0]
    position = here_ref[1]
    zero = jnp.zeros((WIDE, WIDE), bf16)
    odd = (position & 1) == 1
    pair = position >> 1
    carries = []
    for h in heads:
        came = []
        for m, options in enumerate(entries):
            entry = zero
            for j, ref in enumerate(options):
                mine = ((pair >> m) & 1 == 1) & ((pair & ((1 << m) - 1)) == j)
                entry = jnp.where(mine, ref[h], entry)
            came.append(entry)
        wide = jnp.concatenate(came, axis=1)
        ahead = mxu(other_ref[h, :, WIDE:], wide).astype(bf16)
        carries.append(jnp.concatenate(
            [jnp.where(odd, other_ref[h, :, :WIDE], zero)]
            + [
                jnp.where(odd, ahead[:, m * WIDE:(m + 1) * WIDE], x) for m, x in enumerate(came)
            ],
            axis=0,
        ))
    for d in range(size):
        toks = aligned(here ^ d, chunk)

        def head(h):
            part = slice(h * WIDE, (h + 1) * WIDE)
            far = jnp.concatenate([term_ref[i, toks, part] for i in range(1, depth)], axis=1)
            total = mxu(far, carries[h - span[0]])
            yield
            out = slice((h - span[0]) * WIDE, (h - span[0] + 1) * WIDE)
            outs[d][:, out] = (total + term_ref[0, toks, part].astype(f32)).astype(bf16)

        together([head(h) for h in heads])


def finish_call(span, size, here, terms, other, entries, after):
    depth, tokens, width = terms.shape
    smem = pl.BlockSpec(memory_space=pltpu.SMEM)
    vmem = pl.BlockSpec(memory_space=pltpu.VMEM)
    shape = [len(e) for e in entries]
    flat = [x for e in entries for x in e]
    after, spaces = waits(after)

    def kernel(*refs):
        used = 3 + len(flat)
        finish_kernel(span, size, shape, *refs[:used], *refs[used + len(after):])

    return pl.pallas_call(
        kernel,
        in_specs=[smem] + [vmem] * (2 + len(flat)) + spaces,
        out_specs=[vmem] * size,
        out_shape=[jax.ShapeDtypeStruct((tokens // size, span[1] * WIDE), bf16)] * size,
        compiler_params=pltpu.CompilerParams(vmem_limit_bytes=FINISH * MEG),
        name="finish",
    )(here, terms, other, *flat, *after)


def gather_kernel(first, heads, sources, place_ref, *refs):
    parts, (out_ref, mark_ref, sems) = refs[:len(sources)], refs[-3:]
    mark_ref[...] = jnp.zeros_like(mark_ref)
    here = place_ref[0]
    copies = []
    for i, (d, ref) in enumerate(zip(sources, parts)):
        col = pl.multiple_of(((here ^ d) * heads + first) * WIDE, WIDE)
        where = out_ref.at[:, pl.ds(col, ref.shape[1])]
        copies.append(pltpu.make_async_copy(ref, where, sems.at[i]))
        copies[-1].start()
    for c in copies:
        c.wait()


def gather_call(first, heads, size, place, parts, before, after):
    sources, parts = zip(*parts)
    count = len(parts)
    vmem = pl.BlockSpec(memory_space=pltpu.VMEM)
    hbm = pl.BlockSpec(memory_space=pltpu.HBM)
    after, spaces = waits(after)
    kept = [] if before is None else [before]

    def kernel(*refs):
        gather_kernel(first, heads, sources, *refs)

    return pl.pallas_call(
        kernel,
        in_specs=[pl.BlockSpec(memory_space=pltpu.SMEM)] + [vmem] * count + [hbm] * len(kept)
        + spaces,
        out_specs=[hbm, vmem],
        out_shape=[
            jax.ShapeDtypeStruct((parts[0].shape[0], heads * size * WIDE), bf16),
            jax.ShapeDtypeStruct((8, WIDE), f32),
        ],
        input_output_aliases={1 + count: 0} if kept else {},
        scratch_shapes=[pltpu.SemaphoreType.DMA((count,))],
        compiler_params=pltpu.CompilerParams(vmem_limit_bytes=GATHER * MEG),
        name="gather",
    )(place, *parts, *kept, *after)


ORDER = ("l0", "l1", "p0", "h01", "p1", "h02", "h11", "t0", "f00")
ORDER += ("h12", "t1", "a00", "f10", "b00", "a10", "b10")


def order(groups, steps):
    names = dict(l="local", p="pair", t="stage", h="hop", f="finish", g="gather", a="some", b="rest")
    if steps == 3:
        return [(names[x[0]], int(x[1]), int(x[2:] or 0)) for x in ORDER]
    out = [("local", g, 0) for g in range(groups)] + [("pair", g, 0) for g in range(groups)]
    out += [("hop", g, step) for step in range(1, steps) for g in range(groups)]
    out += [("finish", g, i) for g in range(groups) for i in range(PARTS)]
    return out + [("gather", g, i) for g in range(groups) for i in range(PARTS)]


def per_device(queries, key_rows, value_rows, log_decay, write_rate, level_weights, block_levels):
    size = lax.axis_size("ctx")
    bits = size.bit_length() - 1
    width = lax.axis_size("head")
    position = lax.axis_index("ctx").astype(jnp.int32)
    place = lax.axis_index("head").astype(jnp.int32)
    here = jnp.stack([place, position])
    flag = (position & 1).reshape(1)
    heads = log_decay.shape[1]
    groups = split(heads, SHARES)
    pairs = size // 2
    steps = [(m, j) for m in range(pairs.bit_length() - 1) for j in range(1 << m)]

    def swap(low, array):
        to = list(range(pairs))
        for p in low:
            to[p], to[p + 1] = p + 1, p
        return lax.ppermute(array, "ctx", [(i, 2 * to[i >> 1] + (i & 1)) for i in range(size)])

    runs, others, terms, states, solved = {}, {}, {}, {}, []
    entries = [[] for _ in groups]
    pieces = {}
    after = []

    def local(g):
        runs[g], terms[g], mark, *kept = local_call(
            groups[g], heads, bits, block_levels, level_weights.T, solved[0] if solved else None,
            [log_decay.T, write_rate.T, key_rows], queries, value_rows, after,
        )
        if kept:
            solved.append(kept)
        others[g] = lax.ppermute(runs[g], "ctx", [(i, i ^ 1) for i in range(size)])
        return mark, pltpu.VMEM

    def pair(g):
        states[g] = pair_call(flag, runs[g], others[g], after)
        return states[g][1], pltpu.VMEM

    def hop(g, step):
        m, j = steps[step]
        s, t = states[g]
        if j:
            sent = hop_call(t, None, [entries[g][m][j - 1]], after)
        elif m:
            sent = hop_call(t, s, [e[-1] for e in entries[g]], after)
        else:
            sent = s
        if j == 0:
            entries[g].append([])
        low = [p for p in range(pairs) if p % (2 << m) == (1 << m) + j - 1]
        entries[g][m].append(swap(low, sent))
        return sent, pltpu.VMEM

    def stage(g):
        terms[g] = stage_call(terms[g], after)
        return terms[g], pltpu.VMEM

    def span_of(g, part):
        return split(groups[g][1], (1,) * PARTS)[part]

    def finish(g, part):
        outs = finish_call(
            span_of(g, part), width, here, terms[g], others[g], entries[g], after
        )
        for d in range(width):
            pairing = [(i, i ^ d) for i in range(width)]
            pieces[g, part, d] = outs[d] if d == 0 else lax.ppermute(outs[d], "head", pairing)
        return outs[0], pltpu.VMEM

    def gather(g, part, out, ds):
        parts = [(d, pieces[g, part, d]) for d in ds]
        first = groups[g][0] + span_of(g, part)[0]
        return gather_call(first, heads, width, place.reshape(1), parts, out, after)

    out = None
    for name, g, step in order(len(groups), len(steps)):
        if name == "local":
            token = local(g)
        elif name == "pair":
            token = pair(g)
            hop(g, 0)
        elif name == "stage":
            token = stage(g)
        elif name == "hop":
            token = hop(g, step)
        elif name == "finish":
            token = finish(g, step)
        else:
            cut = width - 1
            ds = dict(some=range(cut), rest=range(cut, width)).get(name, range(width))
            out, mark = gather(g, step, out, ds)
            token = mark, pltpu.VMEM
        after = [token]
    return out


def solution(mesh):
    wide = P("ctx", "head")
    return jax.shard_map(
        per_device,
        mesh=mesh,
        in_specs=(wide, wide, wide, wide, wide, wide, P("ctx")),
        out_specs=P(("ctx", "head"), None),
        check_vma=False,
    )
```
